512 devices in a mesh: dp: 8 (over x, y_lo), vseq: 32 (over z, y_hi), aseq: 2 (over core).
Axes of the slice: x: 4, y: 8 (y_hi: 4, y_lo: 2; y = y_hi * 2 + y_lo), z: 8, core: 2. Of those that a mesh axis runs over, the one named last changes fastest.
Arguments:
- video_query: bfloat16 [8, 8192, 1536], P('dp', ('vseq', 'aseq')), may hold values from -6 to 6
- video_key: bfloat16 [8, 8192, 1536], P('dp', ('vseq', 'aseq')), may hold values from -6 to 6
- video_value: bfloat16 [8, 8192, 1536], P('dp', ('vseq', 'aseq')), may hold values from -6 to 6
- video_grad: bfloat16 [8, 8192, 1536], P('dp', ('vseq', 'aseq')), may hold values from -6 to 6
- audio_query: bfloat16 [8, 128, 1536], P('dp', 'vseq'), may hold values from -6 to 6
- audio_key: bfloat16 [8, 128, 1536], P('dp', 'vseq'), may hold values from -6 to 6
- audio_value: bfloat16 [8, 128, 1536], P('dp', 'vseq'), may hold values from -6 to 6
- audio_grad: bfloat16 [8, 128, 1536], P('dp', 'vseq'), may hold values from -6 to 6
- video_pos: int32 [8, 8192], P('dp', ('vseq', 'aseq')), may hold values from 0 to 8191
- audio_pos: int32 [8, 128], P('dp', 'vseq'), may hold values from 0 to 8191
- video_len: int32 [8], P('dp'), may hold values from 4096 to 8192
- audio_len: int32 [8], P('dp'), may hold values from 64 to 128
- gain_vq: float32 [1536], replicated, may hold values from 0.1 to 1.9
- gain_vk: float32 [1536], replicated, may hold values from 0.1 to 1.9
- gain_aq: float32 [1536], replicated, may hold values from 0.1 to 1.9
- gain_ak: float32 [1536], replicated, may hold values from 0.1 to 1.9
Outputs:
- grad_video_query: bfloat16 [8, 8192, 1536], P('dp', ('vseq', 'aseq'))
- grad_video_key: bfloat16 [8, 8192, 1536], P('dp', ('vseq', 'aseq'))
- grad_video_value: bfloat16 [8, 8192, 1536], P('dp', ('vseq', 'aseq'))
- grad_audio_query: bfloat16 [8, 128, 1536], P('dp', 'vseq')
- grad_audio_key: bfloat16 [8, 128, 1536], P('dp', 'vseq')
- grad_audio_value: bfloat16 [8, 128, 1536], P('dp', 'vseq')
- grad_gain_vq: float32 [1536], replicated
- grad_gain_vk: float32 [1536], replicated
- grad_gain_aq: float32 [1536], replicated
- grad_gain_ak: float32 [1536], replicated
The draws below stay inside these ranges and needn't reach their ends.
All inputs are finite; a program needn't handle non-finite values.
Results may differ from the reference program's by a relative error of at most 0.013.
The reference program's roundings to bfloat16 on the way count: a program that leaves them out, or rounds other values in their place, can miss the bound.
Values may be sent and summed in bfloat16 or wider, within the bound.
No kernel may reach another device: no remote copies, remote signals or barrier semaphores. Data moves between devices by JAX's collectives and lax.ppermute only.
A program may use at most 64 MiB of HBM per device.

```python
import jax
import jax.numpy as jnp
from jax import lax

H = 12
DH = 128
CLIPS = 8
VTOK = 8192
ATOK = 128
F = 1536


def plant(values, rng, least, high):
    dims = values.shape
    spot = [jax.random.randint(jax.random.fold_in(rng, axis), (), 0, dims[axis]) for axis in range(len(dims))]
    values = values.at[tuple(spot)].set(least)
    longest = dims.index(max(dims))
    spot[longest] = (spot[longest] + 1) % dims[longest]
    return values.at[tuple(spot)].set(high)


def block_scale(rng, shape, cuts, smallest, high):
    loudness, own = 1.0, jax.random.fold_in(rng, 6)
    for position, shards_of in cuts:
        steps = jnp.exp(jax.random.uniform(jax.random.fold_in(own, position), (shards_of,), jnp.float32, smallest / len(cuts), high / len(cuts)))
        loudness = loudness * jnp.repeat(steps, shape[position] // shards_of).reshape([-1 if axis == position else 1 for axis in range(len(shape))])
    return loudness


def scatter_about(stream_key, dims, spread, limit, cuts=(), held_as=jnp.bfloat16):
    values = jax.random.normal(stream_key, dims, jnp.float32) * spread
    if len(cuts) > 0:
        values = block_scale(stream_key, dims, cuts, -0.22, 0.18) * values
    return jnp.clip(values, min=-limit, max=limit).astype(held_as)


def setup_inputs(seed: int = 0) -> dict:
    splits = jax.random.split(jax.random.key(seed), 17)
    video_query = scatter_about(splits[0], (CLIPS, VTOK, F), 1.0, 6.0, ((0, 8), (1, 64)))
    video_key = scatter_about(splits[1], (CLIPS, VTOK, F), 1.0, 6.0, ((0, 8), (1, 64)))
    video_value = scatter_about(splits[2], (CLIPS, VTOK, F), 1.0, 6.0, ((0, 8), (1, 64)))
    video_grad = scatter_about(splits[3], (CLIPS, VTOK, F), 1.0, 6.0, ((0, 8), (1, 64)))
    audio_query = scatter_about(splits[4], (CLIPS, ATOK, F), 1.0, 6.0, ((0, 8), (1, 32)))
    audio_key = scatter_about(splits[5], (CLIPS, ATOK, F), 1.0, 6.0, ((0, 8), (1, 32)))
    audio_value = scatter_about(splits[6], (CLIPS, ATOK, F), 1.0, 6.0, ((0, 8), (1, 32)))
    audio_grad = scatter_about(splits[7], (CLIPS, ATOK, F), 1.0, 6.0, ((0, 8), (1, 32)))
    video_pos = plant(jax.random.randint(splits[8], (CLIPS, VTOK), 0, VTOK), jax.random.fold_in(splits[8], 1), 0, VTOK - 1).astype(jnp.int32)
    audio_pos = plant(jax.random.randint(splits[9], (CLIPS, ATOK), 0, VTOK), jax.random.fold_in(splits[9], 1), 0, VTOK - 1).astype(jnp.int32)
    video_len = plant(jax.random.randint(splits[10], (CLIPS,), VTOK // 2, VTOK + 1), jax.random.fold_in(splits[10], 1), VTOK // 2, VTOK).astype(jnp.int32)
    audio_len = plant(jax.random.randint(splits[11], (CLIPS,), ATOK // 2, ATOK + 1), jax.random.fold_in(splits[11], 1), ATOK // 2, ATOK).astype(jnp.int32)
    gain_vq = jnp.clip(1.0 + 0.18 * jax.random.normal(splits[12], (F,), jnp.float32), 0.1, 1.9)
    gain_vk = jnp.clip(1.0 + 0.18 * jax.random.normal(splits[13], (F,), jnp.float32), 0.1, 1.9)
    gain_aq = jnp.clip(1.0 + 0.18 * jax.random.normal(splits[14], (F,), jnp.float32), 0.1, 1.9)
    gain_ak = jnp.clip(1.0 + 0.18 * jax.random.normal(splits[15], (F,), jnp.float32), 0.1, 1.9)
    return dict(video_query=video_query, video_key=video_key, video_value=video_value, video_grad=video_grad, audio_query=audio_query, audio_key=audio_key, audio_value=audio_value, audio_grad=audio_grad, video_pos=video_pos, audio_pos=audio_pos, video_len=video_len, audio_len=audio_len, gain_vq=gain_vq, gain_vk=gain_vk, gain_aq=gain_aq, gain_ak=gain_ak)


EPS = 1e-06
THETA = 10000.0

def norm_rope(rows, gain, pos):
    count = rows.shape[0]
    heads = rows.astype(jnp.float32).reshape(count, H, DH)
    scaled = heads * lax.rsqrt(lax.optimization_barrier(jnp.mean(heads * heads, axis=-1, keepdims=True)) + EPS)
    scaled = scaled * gain.astype(jnp.float32).reshape(H, DH)
    half = DH // 2
    freqs = THETA ** (-jnp.arange(half, dtype=jnp.float32) / half)
    angles = pos.astype(jnp.float32)[:, None] * freqs[None, :]
    cosine = jnp.cos(angles)[:, None, :]
    sine = jnp.sin(angles)[:, None, :]
    first = scaled[:, :, :half]
    second = scaled[:, :, half:]
    turned = jnp.concatenate([first * cosine - second * sine, second * cosine + first * sine], axis=-1)
    return turned.reshape(count, H * DH)

def attend_back(query, key, value, cotangent, key_mask):
    scale = DH ** (-0.5)
    heads_q = query.astype(jnp.float32).reshape(query.shape[0], H, DH)
    heads_k = key.astype(jnp.float32).reshape(key.shape[0], H, DH)
    heads_v = value.astype(jnp.float32).reshape(value.shape[0], H, DH)
    heads_c = cotangent.astype(jnp.float32).reshape(cotangent.shape[0], H, DH)
    scores = jnp.einsum('qhd,khd->hqk', heads_q, heads_k) * scale
    expd = jnp.exp(scores) * key_mask[None, None, :]
    prob = expd / lax.optimization_barrier(jnp.sum(expd, axis=-1, keepdims=True))
    prob_low = lax.optimization_barrier(prob.astype(jnp.bfloat16)).astype(jnp.float32)
    dprob = jnp.einsum('qhd,khd->hqk', heads_c, heads_v)
    delta = lax.optimization_barrier(jnp.sum(prob * dprob, axis=-1, keepdims=True))
    dscore = lax.optimization_barrier((prob * (dprob - delta)).astype(jnp.bfloat16)).astype(jnp.float32)
    dquery = jnp.einsum('hqk,khd->qhd', dscore, heads_k) * scale
    dkey = jnp.einsum('hqk,qhd->khd', dscore, heads_q) * scale
    dvalue = jnp.einsum('hqk,qhd->khd', prob_low, heads_c)
    return (dquery.reshape(query.shape[0], H * DH), dkey.reshape(key.shape[0], H * DH), dvalue.reshape(key.shape[0], H * DH))

def one_clip(video_query, video_key, video_value, video_grad, audio_query, audio_key, audio_value, audio_grad, video_pos, audio_pos, video_len, audio_len, gain_vq, gain_vk, gain_aq, gain_ak):
    video_mask = (jnp.arange(VTOK, dtype=jnp.int32) < video_len).astype(jnp.float32)
    audio_mask = (jnp.arange(ATOK, dtype=jnp.int32) < audio_len).astype(jnp.float32)
    video_cot = video_grad * video_mask.astype(jnp.bfloat16)[:, None]
    audio_cot = audio_grad * audio_mask.astype(jnp.bfloat16)[:, None]
    normed_vq, back_vq = jax.vjp(lambda rows, gain: norm_rope(rows, gain, video_pos), video_query, gain_vq)
    normed_vk, back_vk = jax.vjp(lambda rows, gain: norm_rope(rows, gain, video_pos), video_key, gain_vk)
    normed_aq, back_aq = jax.vjp(lambda rows, gain: norm_rope(rows, gain, audio_pos), audio_query, gain_aq)
    normed_ak, back_ak = jax.vjp(lambda rows, gain: norm_rope(rows, gain, audio_pos), audio_key, gain_ak)
    dq_video, dk_audio, dv_audio = attend_back(normed_vq.astype(jnp.bfloat16), normed_ak.astype(jnp.bfloat16), audio_value, video_cot, audio_mask)
    dq_audio, dk_video, dv_video = attend_back(normed_aq.astype(jnp.bfloat16), normed_vk.astype(jnp.bfloat16), video_value, audio_cot, video_mask)
    grad_vq, part_vq = back_vq(dq_video)
    grad_vk, part_vk = back_vk(dk_video)
    grad_aq, part_aq = back_aq(dq_audio)
    grad_ak, part_ak = back_ak(dk_audio)
    return (grad_vq.astype(jnp.bfloat16), grad_vk.astype(jnp.bfloat16), dv_video.astype(jnp.bfloat16), grad_aq.astype(jnp.bfloat16), grad_ak.astype(jnp.bfloat16), dv_audio.astype(jnp.bfloat16), part_vq, part_vk, part_aq, part_ak)

def reference(video_query, video_key, video_value, video_grad, audio_query, audio_key, audio_value, audio_grad, video_pos, audio_pos, video_len, audio_len, gain_vq, gain_vk, gain_aq, gain_ak):

    def per_clip(items):
        return one_clip(items[0], items[1], items[2], items[3], items[4], items[5], items[6], items[7], items[8], items[9], items[10], items[11], gain_vq, gain_vk, gain_aq, gain_ak)
    results = lax.map(per_clip, (video_query, video_key, video_value, video_grad, audio_query, audio_key, audio_value, audio_grad, video_pos, audio_pos, video_len, audio_len))
    return (results[0], results[1], results[2], results[3], results[4], results[5], lax.optimization_barrier(jnp.sum(results[6], axis=0)), lax.optimization_barrier(jnp.sum(results[7], axis=0)), lax.optimization_barrier(jnp.sum(results[8], axis=0)), lax.optimization_barrier(jnp.sum(results[9], axis=0)))
```

```python
import functools

import jax
import jax.numpy as jnp
import numpy as np
from jax import lax
from jax.experimental import pallas as pl
from jax.experimental.pallas import tpu as pltpu
from jax.sharding import PartitionSpec as P

H = 12
DH = 128
HALF = DH // 2
EPS = 1e-06
THETA = 10000.0
SCALE = DH ** (-0.5)
BF = jnp.bfloat16
F32 = jnp.float32
VMEM_LIMIT = 48 * 1024 * 1024


def frequencies():
    freqs = np.power(np.float64(THETA), -(np.arange(HALF, dtype=np.float64) / HALF))
    return jnp.asarray(np.tile(freqs.astype(np.float32), 2).reshape(1, DH))


def sin_cos(angles):
    turns = jnp.floor(angles * F32(2.0 / np.pi) + 0.5)
    rest = angles - turns * F32(1.5703125)
    rest = rest - turns * F32(4.837512969970703125e-4)
    rest = rest - turns * F32(7.54978995489188216e-8)
    sq = rest * rest
    sine = rest + rest * sq * (
        F32(-1.6666654611e-1) + sq * (F32(8.3321608736e-3) + sq * F32(-1.9515295891e-4))
    )
    cosine = (
        1.0
        - 0.5 * sq
        + sq * sq * (F32(4.166664568298827e-2) + sq * (F32(-1.388731625493765e-3) + sq * F32(2.443315711809948e-5)))
    )
    quarter = turns.astype(jnp.int32)
    odd = (quarter & 1) == 1
    flip = (quarter & 2) == 2
    base_s = jnp.where(odd, cosine, sine)
    base_c = jnp.where(odd, -sine, cosine)
    return jnp.where(flip, -base_s, base_s), jnp.where(flip, -base_c, base_c)


def rotary_tables(pos, freqs):
    sine, cosine = sin_cos(pos * freqs)
    lane = lax.broadcasted_iota(jnp.int32, sine.shape, 1)
    return cosine, jnp.where(lane < HALF, -sine, sine)


def swap(rows):
    return pltpu.roll(rows, HALF, 1)


def unit(rows):
    scale = lax.rsqrt(jnp.sum(rows * rows, axis=-1, keepdims=True) * (1.0 / DH) + EPS)
    return rows * scale, scale


def turn(unit_rows, gain, cosine, sine):
    scaled = unit_rows * gain
    return (scaled * cosine + swap(scaled) * sine).astype(BF)


def turn_back(grad, cosine, sine):
    return grad * cosine - swap(grad) * sine


def norm_back(scaled_grad, unit_rows, scale, gain):
    inner = scaled_grad * gain
    mean = jnp.sum(inner * unit_rows, axis=-1, keepdims=True) * (1.0 / DH)
    return scale * (inner - unit_rows * mean)


def low_rows(shape):
    return (lax.broadcasted_iota(jnp.int32, shape, 0) & 7) < 4


def part_rows(both):
    left, right = both[:DH], both[DH:]
    low = low_rows(left.shape)
    one = jnp.where(low, left, pltpu.roll(right, 4, 0))
    two = jnp.where(low, pltpu.roll(left, DH - 4, 0), right)
    return one, two


def join_rows(one, two):
    low = low_rows(one.shape)
    left = jnp.where(low, one, pltpu.roll(two, 4, 0))
    right = jnp.where(low, pltpu.roll(one, DH - 4, 0), two)
    return left, right


def audio_index():
    row = lax.broadcasted_iota(jnp.int32, (DH, DH), 0)
    inside = row & 7
    return jnp.where(inside < 4, 0, 60) + (row >> 3) * 4 + inside


def dot_nt(a, b):
    return lax.dot_general(a, b, (((1,), (1,)), ((), ())), preferred_element_type=F32)


def dot_tn(a, b):
    return lax.dot_general(a, b, (((0,), (0,)), ((), ())), preferred_element_type=F32)


def dot_nn(a, b):
    return lax.dot_general(a, b, (((1,), (0,)), ((), ())), preferred_element_type=F32)


def lanes(head):
    return pl.ds(pl.multiple_of(head * DH, DH), DH)


def first_kernel(
    vlen, alen, own, other, vq, vk, vv, vc, vpos, freqs, gains,
    grad_vq, sums, expo, dprob, raw_aq, low_ac, tables, part_own, part_other,
):
    core = lax.axis_index("aseq")
    place = lax.axis_index("vseq") * 2 + core
    front = core == 0

    def gathered(columns):
        mine, others = own[:, columns], other[:, columns]
        qk = jnp.where(front, mine, others).astype(F32)
        vc = jnp.where(front, others, mine).astype(F32)
        return qk, vc

    row = lax.broadcasted_iota(jnp.int32, (DH, DH), 0)
    lane = lax.broadcasted_iota(jnp.int32, (DH, DH), 1)
    apos, _ = part_rows(own[:, H * DH :].astype(F32))
    apos = jnp.where(lane < HALF, apos * 64.0, apos)
    apos = apos + swap(apos)
    pos = jnp.transpose(jnp.broadcast_to(vpos[...].astype(F32), (DH, DH)))
    tables[0], tables[1] = rotary_tables(pos, freqs[...])
    tables[2], tables[3] = rotary_tables(apos, freqs[...])
    tables[4] = (row + place * DH < vlen[0]).astype(F32)
    tables[5] = (audio_index() < alen[0]).astype(F32)
    sums[...] = jnp.zeros(sums.shape, F32)

    def one_head(head):
        columns = lanes(head)
        cos_v, sin_v, cos_a, sin_a = tables[0], tables[1], tables[2], tables[3]
        mask_v, mask_a = tables[4], tables[5]
        gain_vq, gain_vk = gains[pl.ds(head, 1), :], gains[pl.ds(H + head, 1), :]
        gain_aq, gain_ak = gains[pl.ds(2 * H + head, 1), :], gains[pl.ds(3 * H + head, 1), :]
        qk, vc_audio = gathered(columns)
        aq, ak = part_rows(qk)
        av, ac = part_rows(vc_audio)
        av = av.astype(BF)
        ac = (ac * mask_a).astype(BF)
        raw_aq[:, columns] = aq.astype(BF)
        low_ac[:, columns] = ac
        unit_ak, _ = unit(ak)
        low_ak = turn(unit_ak, gain_ak, cos_a, sin_a)
        unit_aq, _ = unit(aq)
        low_aq = turn(unit_aq, gain_aq, cos_a, sin_a)
        unit_vk, _ = unit(vk[:, columns].astype(F32))
        low_vk = turn(unit_vk, gain_vk, cos_v, sin_v)
        cross = jnp.exp(dot_nt(low_vk, low_aq) * SCALE) * mask_v
        cross_dprob = dot_nt(vv[:, columns], ac)
        expo[head] = cross
        dprob[head] = cross_dprob
        sums[pl.ds(head, 1), :] = jnp.sum(cross, axis=0, keepdims=True)
        sums[pl.ds(H + head, 1), :] = jnp.sum(cross * cross_dprob, axis=0, keepdims=True)
        unit_vq, scale_vq = unit(vq[:, columns].astype(F32))
        low_vq = turn(unit_vq, gain_vq, cos_v, sin_v)
        cot = (vc[:, columns].astype(F32) * mask_v).astype(BF)
        expd = jnp.exp(dot_nt(low_ak, low_vq) * SCALE) * mask_a
        prob = expd * (1.0 / jnp.sum(expd, axis=0, keepdims=True))
        dp = dot_nt(av, cot)
        delta = jnp.sum(prob * dp, axis=0, keepdims=True)
        dscore = (prob * (dp - delta)).astype(BF)
        dq = dot_tn(dscore, low_ak) * SCALE
        dk = dot_nn(dscore, low_vq) * SCALE
        dv = dot_nn(prob.astype(BF), cot)
        back = turn_back(dq, cos_v, sin_v)
        grad_vq[:, columns] = norm_back(back, unit_vq, scale_vq, gain_vq).astype(BF)
        sum_vq = jnp.sum(back * unit_vq, axis=0, keepdims=True)
        sum_ak = jnp.sum(turn_back(dk, cos_a, sin_a) * unit_ak, axis=0, keepdims=True)
        return dk, dv, sum_vq, sum_ak

    for half, part in enumerate((part_own, part_other)):
        base = lax.rem(core + half, 2) * (H // 2)
        part[32] = jnp.zeros(part.shape[1:], F32)

        def pair(step, carry, base=base, part=part):
            found = [one_head(base + 2 * step + e) for e in range(2)]
            for array in range(2):
                left, right = join_rows(found[0][array], found[1][array])
                rows = pl.ds(pl.multiple_of((array * 3 + step) * 8, 8), 8)
                part[0:16, rows, :] = left.reshape(16, 8, DH)
                part[16:32, rows, :] = right.reshape(16, 8, DH)
            for e in range(2):
                part[32, pl.ds(2 * step + e, 1), :] = found[e][2]
                part[32, pl.ds(6 + 2 * step + e, 1), :] = found[e][3]
            return carry

        lax.fori_loop(0, 3, pair, 0)


def second_kernel(
    totals, vk, expo, dprob, raw_aq, low_ac, tables, gains,
    grad_vk, grad_vv, part_own, part_other, sums, deltas,
):
    core = lax.axis_index("aseq")
    whole = jnp.sum(totals[...], axis=0)
    sums[...] = whole
    deltas[...] = 1.0 / whole

    def one_head(head):
        columns = lanes(head)
        cos_v, sin_v, cos_a, sin_a = tables[0], tables[1], tables[2], tables[3]
        gain_vk, gain_aq = gains[pl.ds(H + head, 1), :], gains[pl.ds(2 * H + head, 1), :]
        inverse = deltas[pl.ds(head, 1), :]
        delta = sums[pl.ds(H + head, 1), :] * inverse
        prob = expo[head] * inverse
        dscore = (prob * (dprob[head] - delta)).astype(BF)
        unit_aq, _ = unit(raw_aq[:, columns].astype(F32))
        low_aq = turn(unit_aq, gain_aq, cos_a, sin_a)
        unit_vk, scale_vk = unit(vk[:, columns].astype(F32))
        low_vk = turn(unit_vk, gain_vk, cos_v, sin_v)
        dq = dot_tn(dscore, low_vk) * SCALE
        dk = dot_nn(dscore, low_aq) * SCALE
        grad_vv[:, columns] = dot_nn(prob.astype(BF), low_ac[:, columns]).astype(BF)
        back = turn_back(dk, cos_v, sin_v)
        grad_vk[:, columns] = norm_back(back, unit_vk, scale_vk, gain_vk).astype(BF)
        sum_vk = jnp.sum(back * unit_vk, axis=0, keepdims=True)
        sum_aq = jnp.sum(turn_back(dq, cos_a, sin_a) * unit_aq, axis=0, keepdims=True)
        return dq, sum_vk, sum_aq

    for half, part in enumerate((part_own, part_other)):
        base = lax.rem(core + half, 2) * (H // 2)
        part[32] = jnp.zeros(part.shape[1:], F32)

        def pair(step, carry, base=base, part=part):
            found = [one_head(base + 2 * step + e) for e in range(2)]
            left, right = join_rows(found[0][0], found[1][0])
            rows = pl.ds(pl.multiple_of(step * 8, 8), 8)
            part[0:16, rows, :] = left.reshape(16, 8, DH)
            part[16:32, rows, :] = right.reshape(16, 8, DH)
            for e in range(2):
                part[32, pl.ds(12 + 2 * step + e, 1), :] = found[e][1]
                part[32, pl.ds(18 + 2 * step + e, 1), :] = found[e][2]
            return carry

        lax.fori_loop(0, 3, pair, 0)


def merge_kernel(first, first_got, second, second_got, out):
    gain_rows = first[32, 0:24, :] + first_got[32, 0:24, :] + second[32, 0:24, :] + second_got[32, 0:24, :]

    def block(v, carry):
        out[v, 0:48, :] = (first[v] + first_got[v]).astype(BF)
        tail = jnp.concatenate([second[v] + second_got[v], gain_rows], axis=0)
        out[v, 48:96, :] = tail.astype(BF)
        return carry

    lax.fori_loop(0, 32, block, 0, unroll=4)


def third_kernel(apos, got, aq, ak, freqs, gains, out, gain_out):
    core = lax.axis_index("aseq")
    acc = got[0].astype(F32)
    for v in range(1, 32):
        acc = acc + got[v].astype(F32)
    gain_out[...] = acc[72:96]
    inside = lax.broadcasted_iota(jnp.int32, (8, DH), 0) & 3
    pos = jnp.where(inside < 2, jnp.where(inside == 0, apos[0, 0], apos[0, 1]), jnp.where(inside == 2, apos[0, 2], apos[0, 3]))
    cosine, sine = rotary_tables(pos.astype(F32), freqs[...])
    low = low_rows((8, DH))

    def rows_back(ref, gain_at, grad, at):
        first = core * (H // 2) + 2 * at
        rows = jnp.concatenate([ref[:, lanes(first)].astype(F32), ref[:, lanes(first + 1)].astype(F32)], axis=0)
        gain = jnp.where(low, gains[pl.ds(gain_at * H + first, 1), :], gains[pl.ds(gain_at * H + first + 1, 1), :])
        unit_rows, scale = unit(rows)
        return norm_back(turn_back(grad, cosine, sine), unit_rows, scale, gain)

    for at in range(3):
        dk, dv, dq = (acc[8 * (3 * array + at) : 8 * (3 * array + at) + 8] for array in range(3))
        dq = rows_back(aq, 2, dq, at)
        dk = rows_back(ak, 3, dk, at)
        left = jnp.where(low, dq, pltpu.roll(dk, 4, 0))
        right = jnp.where(low, pltpu.roll(dq, 4, 0), dk)
        out[:, 2 * at * DH : (2 * at + 1) * DH] = jnp.concatenate([left, dv], axis=0).astype(BF)
        out[:, (2 * at + 1) * DH : (2 * at + 2) * DH] = jnp.concatenate([right, pltpu.roll(dv, 4, 0)], axis=0).astype(BF)


def last_kernel(own, other, gains, grad_aq, grad_ak, grad_av, sum_vq, sum_vk, sum_aq, sum_ak):
    front = lax.axis_index("aseq") == 0
    mine, others = own[...].astype(F32), other[...].astype(F32)
    width = mine.shape[1]
    for at, value in enumerate((jnp.where(front, mine, others), jnp.where(front, others, mine))):
        columns = slice(at * width, (at + 1) * width)
        grad_aq[:, columns] = value[0:4].astype(BF)
        grad_ak[:, columns] = value[4:8].astype(BF)
        grad_av[:, columns] = value[8:12].astype(BF)
    for half in range(2):
        total = gains[half]
        for d in range(1, gains.shape[0] // 2):
            total = total + gains[2 * d + half]
        for at, ref in enumerate((sum_vq, sum_ak, sum_vk, sum_aq)):
            ref[6 * half : 6 * half + 6, :] = total[6 * at : 6 * at + 6]


def call(kernel, name, outs, ins, smem=0, scratch=()):
    return pl.pallas_call(
        kernel,
        name=name,
        out_shape=[jax.ShapeDtypeStruct(shape, dtype) for shape, dtype in outs],
        in_specs=[pl.BlockSpec(memory_space=pltpu.SMEM)] * smem
        + [pl.BlockSpec(memory_space=pltpu.VMEM)] * (len(ins) - smem),
        out_specs=[pl.BlockSpec(memory_space=pltpu.VMEM)] * len(outs),
        scratch_shapes=list(scratch),
        compiler_params=pltpu.CompilerParams(vmem_limit_bytes=VMEM_LIMIT),
    )(*ins)


def to_all(rows, axes, count):
    spread = jnp.broadcast_to(rows[None], (count,) + rows.shape)
    return lax.all_to_all(spread, axes, 0, 0, tiled=True)


def local(
    video_query, video_key, video_value, video_grad,
    audio_query, audio_key, audio_value, audio_grad,
    video_pos, audio_pos, video_len, audio_len,
    gain_vq, gain_vk, gain_aq, gain_ak,
):
    F = H * DH
    core = lax.axis_index("aseq")
    groups = lax.axis_size("vseq")
    clips = lax.axis_size("dp")
    exchange = functools.partial(lax.ppermute, axis_name="aseq", perm=[(0, 1), (1, 0)])
    freqs = frequencies()
    gains = jnp.concatenate([gain_vq, gain_vk, gain_aq, gain_ak]).reshape(4 * H, DH)
    mine = jnp.where(
        core == 0,
        jnp.concatenate([audio_query[0], audio_key[0]], axis=0),
        jnp.concatenate([audio_value[0], audio_grad[0]], axis=0),
    )
    places = jnp.tile(audio_pos[0], 2)[:, None]
    lane = jnp.arange(DH, dtype=jnp.int32)[None, :]
    places = jnp.where(lane < HALF, places >> 6, places & 63).astype(BF)
    payload = jnp.concatenate([mine, places], axis=1)
    own = to_all(payload, "vseq", groups).reshape(groups * 8, F + DH)
    other = exchange(own)

    block = (DH, F)
    square = (H, DH, DH)
    grad_vq, sums, expo, dprob, raw_aq, low_ac, tables, first, first_send = call(
        first_kernel,
        "first",
        [
            (block, BF), ((2 * H, DH), F32), (square, F32), (square, F32), (block, BF), (block, BF),
            ((6, DH, DH), F32), ((groups + 1, 48, DH), F32), ((groups + 1, 48, DH), F32),
        ],
        [
            video_len, audio_len, own, other, video_query[0], video_key[0], video_value[0], video_grad[0],
            video_pos, freqs, gains,
        ],
        smem=2,
    )
    sums = sums + exchange(sums)
    first_got = exchange(first_send)
    totals = to_all(sums, "vseq", groups)
    grad_vk, grad_vv, second, second_send = call(
        second_kernel,
        "second",
        [(block, BF), (block, BF), ((groups + 1, 24, DH), F32), ((groups + 1, 24, DH), F32)],
        [totals, video_key[0], expo, dprob, raw_aq, low_ac, tables, gains],
        scratch=[pltpu.VMEM((2 * H, DH), F32), pltpu.VMEM((2 * H, DH), F32)],
    )
    second_got = exchange(second_send)
    (merged,) = call(
        merge_kernel, "merge", [((groups, 96, DH), BF)], [first, first_got, second, second_got]
    )
    got = lax.all_to_all(merged, "vseq", 0, 0, tiled=True)
    half, gain_sums = call(
        third_kernel,
        "third",
        [((16, F // 2), BF), ((2 * H, DH), F32)],
        [audio_pos, got, audio_query[0], audio_key[0], freqs, gains],
        smem=1,
    )
    half_got = exchange(half)
    gain_got = to_all(gain_sums, ("dp", "aseq"), 2 * clips)
    grad_aq, grad_ak, grad_av, sum_vq, sum_vk, sum_aq, sum_ak = call(
        last_kernel,
        "last",
        [((4, F), BF)] * 3 + [((H, DH), F32)] * 4,
        [half, half_got, gain_got],
    )
    return (
        grad_vq[None],
        grad_vk[None],
        grad_vv[None],
        grad_aq[None],
        grad_ak[None],
        grad_av[None],
        sum_vq.reshape(F),
        sum_vk.reshape(F),
        sum_aq.reshape(F),
        sum_ak.reshape(F),
    )


def solution(mesh):
    video = P("dp", ("vseq", "aseq"), None)
    audio = P("dp", "vseq", None)
    in_specs = (
        (video,) * 4
        + (audio,) * 4
        + (P("dp", ("vseq", "aseq")), P("dp", "vseq"), P("dp"), P("dp"))
        + (P(),) * 4
    )
    out_specs = (video,) * 3 + (audio,) * 3 + (P(),) * 4
    return jax.shard_map(local, mesh=mesh, in_specs=in_specs, out_specs=out_specs, check_vma=False)
```

```python
import functools

import jax
import jax.numpy as jnp
import numpy as np
from jax import lax
from jax.experimental import pallas as pl
from jax.experimental.pallas import tpu as pltpu
from jax.sharding import PartitionSpec as P

H = 12
DH = 128
HALF = DH // 2
EPS = 1e-06
THETA = 10000.0
SCALE = DH ** (-0.5)
BF = jnp.bfloat16
F32 = jnp.float32
VMEM_LIMIT = 24 * 1024 * 1024
HALF_HEADS = H // 2
WIDTH = HALF_HEADS * DH


def frequencies():
    freqs = np.power(np.float64(THETA), -(np.arange(HALF, dtype=np.float64) / HALF))
    return jnp.asarray(np.tile(freqs.astype(np.float32), 2).reshape(1, DH))


def sin_cos(angles):
    turns = jnp.floor(angles * F32(2.0 / np.pi) + 0.5)
    rest = angles - turns * F32(1.5703125)
    rest = rest - turns * F32(4.837512969970703125e-4)
    rest = rest - turns * F32(7.54978995489188216e-8)
    sq = rest * rest
    sine = rest + rest * sq * (
        F32(-1.6666654611e-1) + sq * (F32(8.3321608736e-3) + sq * F32(-1.9515295891e-4))
    )
    cosine = (
        1.0
        - 0.5 * sq
        + sq * sq * (F32(4.166664568298827e-2) + sq * (F32(-1.388731625493765e-3) + sq * F32(2.443315711809948e-5)))
    )
    quarter = turns.astype(jnp.int32)
    odd = (quarter & 1) == 1
    flip = (quarter & 2) == 2
    base_s = jnp.where(odd, cosine, sine)
    base_c = jnp.where(odd, -sine, cosine)
    return jnp.where(flip, -base_s, base_s), jnp.where(flip, -base_c, base_c)


def rotary_tables(pos, freqs):
    sine, cosine = sin_cos(pos * freqs)
    lane = lax.broadcasted_iota(jnp.int32, sine.shape, 1)
    return cosine, jnp.where(lane < HALF, -sine, sine)


def swap(rows):
    return pltpu.roll(rows, HALF, 1)


def unit(rows):
    scale = lax.rsqrt(jnp.sum(rows * rows, axis=-1, keepdims=True) * (1.0 / DH) + EPS)
    return rows * scale, scale


def turn(unit_rows, gain, cosine, sine):
    scaled = unit_rows * gain
    return (scaled * cosine + swap(scaled) * sine).astype(BF)


def turn_back(grad, cosine, sine):
    return grad * cosine - swap(grad) * sine


def norm_back(scaled_grad, unit_rows, scale, gain):
    inner = scaled_grad * gain
    mean = jnp.sum(inner * unit_rows, axis=-1, keepdims=True) * (1.0 / DH)
    return scale * (inner - unit_rows * mean)


def low_rows(shape):
    return (lax.broadcasted_iota(jnp.int32, shape, 0) & 7) < 4


def part_rows(both):
    left, right = both[:DH], both[DH:]
    low = low_rows(left.shape)
    one = jnp.where(low, left, pltpu.roll(right, 4, 0))
    two = jnp.where(low, pltpu.roll(left, DH - 4, 0), right)
    return one, two


def join_rows(one, two):
    low = low_rows(one.shape)
    left = jnp.where(low, one, pltpu.roll(two, 4, 0))
    right = jnp.where(low, pltpu.roll(one, DH - 4, 0), two)
    return left, right


def audio_index():
    row = lax.broadcasted_iota(jnp.int32, (DH, DH), 0)
    inside = row & 7
    return jnp.where(inside < 4, 0, 60) + (row >> 3) * 4 + inside


def dot_nt(a, b):
    return lax.dot_general(a, b, (((1,), (1,)), ((), ())), preferred_element_type=F32)


def dot_tn(a, b):
    return lax.dot_general(a, b, (((0,), (0,)), ((), ())), preferred_element_type=F32)


def dot_nn(a, b):
    return lax.dot_general(a, b, (((1,), (0,)), ((), ())), preferred_element_type=F32)


def lanes(head):
    return pl.ds(pl.multiple_of(head * DH, DH), DH)


def heads_of(core):
    return core * HALF_HEADS


def fetch(pairs, done):
    copies = [pltpu.make_async_copy(far, near, done.at[at]) for at, (far, near) in enumerate(pairs)]
    for copy in copies:
        copy.start()
    return copies


def finish(copies):
    for copy in copies:
        copy.wait()


def payload_kernel(apos_far, aq_far, ak_far, av_far, ac_far, out, apos, aq, ak, av, ac, done):
    finish(fetch(((apos_far, apos), (aq_far, aq), (ak_far, ak), (av_far, av), (ac_far, ac)), done))
    base = heads_of(lax.axis_index("aseq"))
    for j in range(HALF_HEADS):
        columns = lanes(base + j)
        for at, pair in enumerate(((aq, ak), (av, ac))):
            rows = jnp.concatenate([ref[0, :, columns].astype(F32) for ref in pair], axis=0).astype(BF)
            out[:, 2 * j + at] = jnp.broadcast_to(rows[None], (32, 8, DH))
    inside = lax.broadcasted_iota(jnp.int32, (8, DH), 0) & 3
    lane = lax.broadcasted_iota(jnp.int32, (8, DH), 1)
    pos = own_places(apos, inside)
    pos = jnp.where(lane < HALF, pos >> 6, pos & 63).astype(F32).astype(BF)
    out[:, 2 * HALF_HEADS] = jnp.broadcast_to(pos[None], (32, 8, DH))


def own_places(apos, inside):
    early = jnp.where(inside == 0, apos[0, 0], apos[0, 1])
    late = jnp.where(inside == 2, apos[0, 2], apos[0, 3])
    return jnp.where(inside < 2, early, late)


def send_kernel(vq, vk, vv, vc, out):
    base = heads_of(1 - lax.axis_index("aseq"))
    columns = pl.ds(pl.multiple_of(base * DH, DH), WIDTH)
    for at, ref in enumerate((vq, vk, vv, vc)):
        out[at] = ref[:, columns]


def video_mask(vlen, core):
    place = lax.axis_index("vseq") * 2 + core
    row = lax.broadcasted_iota(jnp.int32, (DH, DH), 0)
    return [(row + where * DH < vlen[0]).astype(F32) for where in (place, place + 1 - 2 * core)]


def video_kernel(
    vlen, vq, vk, vv, vc, got, pos_own, pos_got, freqs, gains,
    queries_far, keys_far, raw_vk_far, unit_vk_far, tables_far,
    queries, keys, raw_vk, unit_vk, tables, done,
):
    core = lax.axis_index("aseq")
    base = heads_of(core)
    masks = video_mask(vlen, core)
    for at, pos in enumerate((pos_own, pos_got)):
        rows = slice(at * DH, (at + 1) * DH)
        spread = jnp.transpose(jnp.broadcast_to(pos[...].astype(F32), (DH, DH)))
        tables[0, rows], tables[1, rows] = rotary_tables(spread, freqs[...])
        tables[2, rows] = masks[at]

    def one_head(j, carry):
        columns = lanes(j)
        own_columns = lanes(base + j)
        for at in range(2):
            rows = slice(at * DH, (at + 1) * DH)
            take = (lambda ref, index: ref[:, own_columns]) if at == 0 else (lambda ref, index: got[index, :, columns])
            cosine, sine, mask = tables[0, rows], tables[1, rows], tables[2, rows]
            query, key = take(vq, 0), take(vk, 1)
            queries[j, 0, rows] = query
            raw_vk[j, rows] = key
            keys[j, 1, rows] = take(vv, 2)
            queries[j, 2, rows] = (take(vc, 3).astype(F32) * mask).astype(BF)
            unit_query, _ = unit(query.astype(F32))
            unit_key, _ = unit(key.astype(F32))
            queries[j, 1, rows] = turn(unit_query, gains[pl.ds(base + j, 1), :], cosine, sine)
            keys[j, 0, rows] = turn(unit_key, gains[pl.ds(H + base + j, 1), :], cosine, sine)
            unit_vk[j, rows] = unit_key
        return carry

    lax.fori_loop(0, HALF_HEADS, one_head, 0)
    finish(
        fetch(
            (
                (queries, queries_far), (keys, keys_far), (raw_vk, raw_vk_far), (unit_vk, unit_vk_far),
                (tables, tables_far),
            ),
            done,
        )
    )


def audio_tables(gathered, freqs, alen):
    lane = lax.broadcasted_iota(jnp.int32, (DH, DH), 1)
    apos, _ = part_rows(gathered[:, 2 * HALF_HEADS].astype(F32).reshape(2 * DH, DH))
    apos = jnp.where(lane < HALF, apos * 64.0, apos)
    apos = apos + swap(apos)
    cosine, sine = rotary_tables(apos, freqs[...])
    return cosine, sine, (audio_index() < alen[0]).astype(F32)


def scores_kernel(alen, vlen, gathered, keys, freqs, gains, sums, tables, mask):
    core = lax.axis_index("aseq")
    base = heads_of(core)
    tables[0], tables[1], tables[2] = audio_tables(gathered, freqs, alen)
    mask[0:DH], mask[DH : 2 * DH] = video_mask(vlen, core)
    found = []
    for j in range(HALF_HEADS):
        aq, _ = part_rows(gathered[:, 2 * j].astype(F32).reshape(2 * DH, DH))
        _, ac = part_rows(gathered[:, 2 * j + 1].astype(F32).reshape(2 * DH, DH))
        rows, _ = unit(aq)
        query = turn(rows, gains[pl.ds(2 * H + base + j, 1), :], tables[0], tables[1])
        cross = jnp.exp(dot_nt(keys[j, 0], query) * SCALE) * mask[...]
        dprob = dot_nt(keys[j, 1], (ac * tables[2]).astype(BF))
        found.append((jnp.sum(cross, axis=0, keepdims=True), jnp.sum(cross * dprob, axis=0, keepdims=True)))
    rows = [pair[0] for pair in found] + [pair[1] for pair in found]
    for at in range(3):
        block = jnp.concatenate(rows[4 * at : 4 * at + 4], axis=0)
        sums[:, at] = jnp.broadcast_to(block[None], (32, 4, DH))


def queries_kernel(
    alen, gathered, freqs, gains, queries_far, keys_far, video_far,
    scores_far, audio_far, tables_far, part_far, gain_far, other_far, grad_own,
    queries, keys, video_tables, scores, audio, tables, part, gain_rows, grad_other, done_in, done_out,
):
    coming = fetch(((video_far, video_tables), (keys_far, keys), (queries_far, queries)), done_in)
    base = heads_of(lax.axis_index("aseq"))
    tables[0], tables[1], tables[2] = audio_tables(gathered, freqs, alen)
    gain_rows[...] = jnp.zeros(gain_rows.shape, F32)
    finish(coming)

    def one_head(j):
        columns = lanes(j)
        cos_v, sin_v, mask_v = video_tables[0], video_tables[1], video_tables[2]
        cos_a, sin_a, mask_a = tables[0], tables[1], tables[2]
        aq, ak = part_rows(gathered[:, 2 * j].astype(F32).reshape(2 * DH, DH))
        av, ac = part_rows(gathered[:, 2 * j + 1].astype(F32).reshape(2 * DH, DH))
        av = av.astype(BF)
        ac = (ac * mask_a).astype(BF)
        unit_aq, _ = unit(aq)
        low_aq = turn(unit_aq, gains[pl.ds(2 * H + base + j, 1), :], cos_a, sin_a)
        unit_ak, _ = unit(ak)
        low_ak = turn(unit_ak, gains[pl.ds(3 * H + base + j, 1), :], cos_a, sin_a)
        scores[j, 0 : 2 * DH] = jnp.exp(dot_nt(keys[j, 0], low_aq) * SCALE) * mask_v
        scores[j, 2 * DH : 4 * DH] = dot_nt(keys[j, 1], ac)
        scores[j, 4 * DH : 5 * DH] = unit_aq
        audio[j, 0] = low_aq
        audio[j, 1] = ac
        rows, cots = queries[j, 1], queries[j, 2]
        expd = jnp.exp(dot_nt(low_ak, rows) * SCALE) * jnp.concatenate([mask_a, mask_a], axis=1)
        prob = expd * (1.0 / jnp.sum(expd, axis=0, keepdims=True))
        dp = dot_nt(av, cots)
        delta = jnp.sum(prob * dp, axis=0, keepdims=True)
        dscore = (prob * (dp - delta)).astype(BF)
        dk = dot_nn(dscore, rows) * SCALE
        dv = dot_nn(prob.astype(BF), cots)
        back = turn_back(dot_tn(dscore, low_ak) * SCALE, cos_v, sin_v)
        unit_vq, scale_vq = unit(queries[j, 0].astype(F32))
        grad = norm_back(back, unit_vq, scale_vq, gains[pl.ds(base + j, 1), :]).astype(BF)
        grad_own[:, columns] = grad[:DH]
        grad_other[:, columns] = grad[DH:]
        gain_rows[pl.ds(j, 1), :] = jnp.sum(back * unit_vq, axis=0, keepdims=True)
        gain_rows[pl.ds(18 + j, 1), :] = jnp.sum(turn_back(dk, cos_a, sin_a) * unit_ak, axis=0, keepdims=True)
        return dk, dv

    def pair(step, carry):
        found = [one_head(2 * step + e) for e in range(2)]
        for array in range(2):
            left, right = join_rows(found[0][array], found[1][array])
            part[0:16, array * 3 + step] = left.reshape(16, 8, DH).astype(BF)
            part[16:32, array * 3 + step] = right.reshape(16, 8, DH).astype(BF)
        return carry

    lax.fori_loop(0, 3, pair, 0)
    finish(
        fetch(
            (
                (scores, scores_far), (audio, audio_far), (tables, tables_far), (part, part_far),
                (gain_rows, gain_far), (grad_other, other_far),
            ),
            done_out,
        )
    )


def back_kernel(
    totals, scores_far, audio_far, keys_far, unit_vk_far, video_far, tables_far, part_far, gain_far, merged,
    scores, audio, keys, unit_vk, video_tables, tables, gain_rows, done,
):
    first = [(scores_far.at[j], scores.at[j]) for j in range(HALF_HEADS)]
    second = [(audio_far.at[j, 0], audio.at[j]) for j in range(HALF_HEADS)]
    third = [(keys_far.at[j, 0], keys.at[j]) for j in range(HALF_HEADS)]
    fourth = [(unit_vk_far.at[j], unit_vk.at[j]) for j in range(HALF_HEADS)]
    order = [pair for head in zip(first, third, second, fourth) for pair in head]
    order[4:4] = [(video_far, video_tables), (tables_far, tables), (gain_far, gain_rows)]
    order.append((part_far, merged.at[:, 3:9]))
    copies = fetch(order, done)
    blocks = [jnp.sum(totals[:, at], axis=0) for at in range(3)]
    rows = [blocks[r // 4][r % 4 : r % 4 + 1] for r in range(2 * HALF_HEADS)]
    found = []
    for j in range(HALF_HEADS):
        finish(copies[:7] if j == 0 else copies[4 * j + 3 : 4 * j + 7])
        inverse = 1.0 / rows[j]
        delta = rows[HALF_HEADS + j] * inverse
        dscore = (scores[j, 0 : 2 * DH] * inverse * (scores[j, 2 * DH : 4 * DH] - delta)).astype(BF)
        dq = dot_tn(dscore, keys[j]) * SCALE
        dk = dot_nn(dscore, audio[j]) * SCALE
        back = turn_back(dk, video_tables[0], video_tables[1])
        gain_rows[6 + j : 7 + j, :] = jnp.sum(back * unit_vk[j], axis=0, keepdims=True)
        back = turn_back(dq, tables[0], tables[1])
        gain_rows[12 + j : 13 + j, :] = jnp.sum(back * scores[j, 4 * DH : 5 * DH], axis=0, keepdims=True)
        found.append(dq)
        if j % 2 == 1:
            left, right = join_rows(found[j - 1], found[j])
            merged[0:16, j // 2] = left.reshape(16, 8, DH).astype(BF)
            merged[16:32, j // 2] = right.reshape(16, 8, DH).astype(BF)
    for at in range(3):
        block = gain_rows[8 * at : 8 * at + 8, :].astype(BF)
        merged[:, 9 + at] = jnp.broadcast_to(block[None], (32, 8, DH))
    finish(copies[-1:])


def keys_kernel(
    totals, scores_far, audio_far, raw_vk_far, video_far, query_far, gains,
    key_own, value_own, other, scores, audio, raw_vk, video_tables, sums, done,
):
    copies = fetch(
        (
            (scores_far.at[:, 0 : 4 * DH], scores), (audio_far, audio), (raw_vk_far, raw_vk),
            (video_far.at[0:2], video_tables), (query_far, other.at[0]),
        ),
        done,
    )
    base = heads_of(lax.axis_index("aseq"))
    for at in range(3):
        sums[4 * at : 4 * at + 4, :] = jnp.sum(totals[:, at], axis=0)
    finish(copies)

    def one_head(j, carry):
        columns = lanes(j)
        cosine, sine = video_tables[0], video_tables[1]
        inverse = 1.0 / sums[pl.ds(j, 1), :]
        delta = sums[pl.ds(HALF_HEADS + j, 1), :] * inverse
        prob = scores[j, 0 : 2 * DH] * inverse
        dscore = (prob * (scores[j, 2 * DH : 4 * DH] - delta)).astype(BF)
        dk = dot_nn(dscore, audio[j, 0]) * SCALE
        dv = dot_nn(prob.astype(BF), audio[j, 1]).astype(BF)
        unit_vk, scale_vk = unit(raw_vk[j].astype(F32))
        gain = gains[pl.ds(H + base + j, 1), :]
        grad = norm_back(turn_back(dk, cosine, sine), unit_vk, scale_vk, gain).astype(BF)
        key_own[:, columns] = grad[:DH]
        value_own[:, columns] = dv[:DH]
        other[1, :, columns] = grad[DH:]
        other[2, :, columns] = dv[DH:]
        return carry

    lax.fori_loop(0, HALF_HEADS, one_head, 0)


def place_kernel(query_own, key_own, value_own, got, grad_vq, grad_vk, grad_vv):
    core = lax.axis_index("aseq")
    own = pl.ds(pl.multiple_of(heads_of(core) * DH, DH), WIDTH)
    other = pl.ds(pl.multiple_of(heads_of(1 - core) * DH, DH), WIDTH)
    for at, (mine, grad) in enumerate(((query_own, grad_vq), (key_own, grad_vk), (value_own, grad_vv))):
        grad[:, own] = mine[...]
        grad[:, other] = got[at]


def audio_kernel(apos_far, aq_far, ak_far, freqs_far, gains_far, after, got, out, gain_out, apos, aq, ak, freqs, gains, done):
    copies = fetch(((apos_far, apos), (aq_far, aq), (ak_far, ak), (freqs_far, freqs), (gains_far, gains)), done)
    base = heads_of(lax.axis_index("aseq"))
    acc = got[0].astype(F32)
    for v in range(1, 32):
        acc = acc + got[v].astype(F32)
    gain_out[...] = jnp.broadcast_to(acc[9:12].reshape(1, 24, DH), gain_out.shape)
    finish(copies)
    pos = own_places(apos, lax.broadcasted_iota(jnp.int32, (8, DH), 0) & 3)
    cosine, sine = rotary_tables(pos.astype(F32), freqs[...])
    low = low_rows((8, DH))

    def rows_back(ref, gain_at, grad, at):
        first = base + 2 * at
        rows = jnp.concatenate([ref[0, :, lanes(first + e)].astype(F32) for e in range(2)], axis=0)
        gain = jnp.where(low, gains[pl.ds(gain_at * H + first, 1), :], gains[pl.ds(gain_at * H + first + 1, 1), :])
        unit_rows, scale = unit(rows)
        return norm_back(turn_back(grad, cosine, sine), unit_rows, scale, gain)

    for at in range(3):
        dq = rows_back(aq, 2, acc[at], at)
        dk = rows_back(ak, 3, acc[3 + at], at)
        dv = acc[6 + at]
        left = jnp.where(low, dq, pltpu.roll(dk, 4, 0))
        right = jnp.where(low, pltpu.roll(dq, 4, 0), dk)
        out[:, 2 * at * DH : (2 * at + 1) * DH] = jnp.concatenate([left, dv], axis=0).astype(BF)
        out[:, (2 * at + 1) * DH : (2 * at + 2) * DH] = jnp.concatenate([right, pltpu.roll(dv, 4, 0)], axis=0).astype(BF)


def last_kernel(own, other, gains, grad_aq, grad_ak, grad_av, sum_vq, sum_vk, sum_aq, sum_ak):
    front = lax.axis_index("aseq") == 0
    mine, others = own[...].astype(F32), other[...].astype(F32)
    for at, value in enumerate((jnp.where(front, mine, others), jnp.where(front, others, mine))):
        columns = slice(at * WIDTH, (at + 1) * WIDTH)
        grad_aq[:, columns] = value[0:4].astype(BF)
        grad_ak[:, columns] = value[4:8].astype(BF)
        grad_av[:, columns] = value[8:12].astype(BF)
    for half in range(2):
        total = gains[half]
        for d in range(1, gains.shape[0] // 2):
            total = total + gains[2 * d + half]
        for at, ref in enumerate((sum_vq, sum_vk, sum_aq, sum_ak)):
            ref[6 * half : 6 * half + 6, :] = total[6 * at : 6 * at + 6]


NEAR, FAR = pltpu.VMEM, pltpu.HBM


def call(kernel, name, outs, ins, smem=0, far=0, scratch=()):
    def shape_of(shape, dtype, space=None):
        return jax.ShapeDtypeStruct(shape, dtype) if space is None else space(shape, dtype)

    ins = [pltpu.with_memory_space_constraint(x, FAR) if smem <= at < smem + far else x for at, x in enumerate(ins)]
    return pl.pallas_call(
        kernel,
        name=name,
        out_shape=[shape_of(*out) for out in outs],
        in_specs=[pl.BlockSpec(memory_space=pltpu.SMEM)] * smem
        + [pl.BlockSpec(memory_space=FAR)] * far
        + [pl.BlockSpec(memory_space=NEAR)] * (len(ins) - smem - far),
        out_specs=[pl.BlockSpec(memory_space=FAR if FAR in out else NEAR) for out in outs],
        scratch_shapes=list(scratch),
        compiler_params=pltpu.CompilerParams(vmem_limit_bytes=VMEM_LIMIT),
    )(*ins)


def local(
    video_query, video_key, video_value, video_grad,
    audio_query, audio_key, audio_value, audio_grad,
    video_pos, audio_pos, video_len, audio_len,
    gain_vq, gain_vk, gain_aq, gain_ak,
):
    F = H * DH
    groups = lax.axis_size("vseq")
    clips = lax.axis_size("dp")
    exchange = functools.partial(lax.ppermute, axis_name="aseq", perm=[(0, 1), (1, 0)])
    to_group = functools.partial(lax.all_to_all, axis_name="vseq", split_axis=0, concat_axis=0, tiled=True)
    freqs = frequencies()
    gains = jnp.concatenate([gain_vq, gain_vk, gain_aq, gain_ak]).reshape(4 * H, DH)
    video = [video_query[0], video_key[0], video_value[0], video_grad[0]]
    half = (DH, WIDTH)
    tiles = (groups, 2 * HALF_HEADS, 8, DH)
    six = (HALF_HEADS, 2 * DH, DH)
    queries_shape, keys_shape = (HALF_HEADS, 3, 2 * DH, DH), (HALF_HEADS, 2, 2 * DH, DH)
    scores_shape, audio_shape = (HALF_HEADS, 5 * DH, DH), (HALF_HEADS, 2, DH, DH)
    video_tables_shape, tables_shape = (3, 2 * DH, DH), (3, DH, DH)
    part_shape, gain_shape = (groups, 6, 8, DH), (24, DH)
    dmas = lambda count: pltpu.SemaphoreType.DMA((count,))

    (payload,) = call(
        payload_kernel,
        "payload",
        [((groups, 2 * HALF_HEADS + 1, 8, DH), BF)],
        [audio_pos, audio_query, audio_key, audio_value, audio_grad],
        far=5,
        scratch=[pltpu.SMEM((1, 4), jnp.int32)] + [pltpu.VMEM((1, 4, F), BF)] * 4 + [dmas(5)],
    )
    gathered = to_group(payload)

    (send,) = call(send_kernel, "send", [((4, DH, WIDTH), BF)], video)
    video_got = exchange(send)
    pos_got = exchange(video_pos)
    queries, keys, raw_vk, unit_vk, video_tables = call(
        video_kernel,
        "video",
        [
            (queries_shape, BF, FAR), (keys_shape, BF, FAR), (six, BF, FAR), (six, F32, FAR),
            (video_tables_shape, F32, FAR),
        ],
        [video_len, *video, video_got, video_pos, pos_got, freqs, gains],
        smem=1,
        scratch=[
            pltpu.VMEM(queries_shape, BF), pltpu.VMEM(keys_shape, BF), pltpu.VMEM(six, BF), pltpu.VMEM(six, F32),
            pltpu.VMEM(video_tables_shape, F32), dmas(5),
        ],
    )

    (sums,) = call(
        scores_kernel,
        "scores",
        [((groups, 3, 4, DH), F32)],
        [audio_len, video_len, gathered, keys, freqs, gains],
        smem=2,
        scratch=[pltpu.VMEM(tables_shape, F32), pltpu.VMEM((2 * DH, DH), F32)],
    )
    totals = to_group(sums)

    far_queries = [queries, keys, video_tables]
    scores, audio, tables, part, gain_part, query_other, query_own = call(
        lambda alen, queries, keys, video, *rest: queries_kernel(alen, *rest[:3], queries, keys, video, *rest[3:]),
        "queries",
        [
            (scores_shape, F32, FAR), (audio_shape, BF, FAR), (tables_shape, F32, FAR), (part_shape, BF, FAR),
            (gain_shape, F32, FAR), (half, BF, FAR), (half, BF),
        ],
        [audio_len, *far_queries, gathered, freqs, gains],
        smem=1,
        far=3,
        scratch=[
            pltpu.VMEM(queries_shape, BF), pltpu.VMEM(keys_shape, BF), pltpu.VMEM(video_tables_shape, F32),
            pltpu.VMEM(scores_shape, F32), pltpu.VMEM(audio_shape, BF), pltpu.VMEM(tables_shape, F32),
            pltpu.VMEM(part_shape, BF), pltpu.VMEM(gain_shape, F32), pltpu.VMEM(half, BF), dmas(3), dmas(6),
        ],
    )

    (merged,) = call(
        lambda *refs: back_kernel(refs[8], *refs[:8], *refs[9:]),
        "back",
        [(tiles, BF)],
        [scores, audio, keys, unit_vk, video_tables, tables, part, gain_part, totals],
        far=8,
        scratch=[
            pltpu.VMEM(scores_shape, F32), pltpu.VMEM((HALF_HEADS, DH, DH), BF), pltpu.VMEM(six, BF),
            pltpu.VMEM(six, F32), pltpu.VMEM(video_tables_shape, F32), pltpu.VMEM(tables_shape, F32),
            pltpu.VMEM(gain_shape, F32), dmas(4 * HALF_HEADS + 4),
        ],
    )
    got = to_group(merged)

    key_own, value_own, other = call(
        lambda *refs: keys_kernel(refs[5], *refs[:5], *refs[6:]),
        "keys",
        [(half, BF), (half, BF), ((3, DH, WIDTH), BF)],
        [scores, audio, raw_vk, video_tables, query_other, totals, gains],
        far=5,
        scratch=[
            pltpu.VMEM((HALF_HEADS, 4 * DH, DH), F32), pltpu.VMEM(audio_shape, BF), pltpu.VMEM(six, BF),
            pltpu.VMEM((2, 2 * DH, DH), F32), pltpu.VMEM((16, DH), F32), dmas(5),
        ],
    )
    other_got = exchange(other)
    grad_vq, grad_vk, grad_vv = call(
        place_kernel, "place", [((DH, F), BF)] * 3, [query_own, key_own, value_own, other_got]
    )

    audio_half, gain_rows = call(
        audio_kernel,
        "audio",
        [((16, WIDTH), BF), ((2 * clips, 24, DH), F32)],
        [audio_pos, audio_query, audio_key, freqs, gains, grad_vv, got],
        far=6,
        scratch=[
            pltpu.SMEM((1, 4), jnp.int32), pltpu.VMEM((1, 4, F), BF), pltpu.VMEM((1, 4, F), BF),
            pltpu.VMEM((1, DH), F32), pltpu.VMEM((4 * H, DH), F32), dmas(5),
        ],
    )
    gain_got = lax.all_to_all(gain_rows, ("dp", "aseq"), 0, 0, tiled=True)
    audio_got = exchange(audio_half)
    grad_aq, grad_ak, grad_av, sum_vq, sum_vk, sum_aq, sum_ak = call(
        last_kernel,
        "last",
        [((4, F), BF)] * 3 + [((H, DH), F32)] * 4,
        [audio_half, audio_got, gain_got],
    )
    return (
        grad_vq[None],
        grad_vk[None],
        grad_vv[None],
        grad_aq[None],
        grad_ak[None],
        grad_av[None],
        sum_vq.reshape(F),
        sum_vk.reshape(F),
        sum_aq.reshape(F),
        sum_ak.reshape(F),
    )


def solution(mesh):
    video = P("dp", ("vseq", "aseq"), None)
    audio = P("dp", "vseq", None)
    in_specs = (
        (video,) * 4
        + (audio,) * 4
        + (P("dp", ("vseq", "aseq")), P("dp", "vseq"), P("dp"), P("dp"))
        + (P(),) * 4
    )
    out_specs = (video,) * 3 + (audio,) * 3 + (P(),) * 4
    return jax.shard_map(local, mesh=mesh, in_specs=in_specs, out_specs=out_specs, check_vma=False)
```

```python
import functools

import jax
import jax.numpy as jnp
import numpy as np
from jax import lax
from jax.experimental import pallas as pl
from jax.experimental.pallas import tpu as pltpu
from jax.sharding import PartitionSpec as P

H = 12
DH = 128
HALF = DH // 2
EPS = 1e-06
THETA = 10000.0
SCALE = DH ** (-0.5)
BF = jnp.bfloat16
F32 = jnp.float32
VMEM_LIMIT = 24 * 1024 * 1024
HALF_HEADS = H // 2
WIDTH = HALF_HEADS * DH


def frequencies():
    freqs = np.power(np.float64(THETA), -(np.arange(HALF, dtype=np.float64) / HALF))
    return jnp.asarray(np.tile(freqs.astype(np.float32), 2).reshape(1, DH))


def sin_cos(angles):
    turns = jnp.floor(angles * F32(2.0 / np.pi) + 0.5)
    rest = angles - turns * F32(1.5703125)
    rest = rest - turns * F32(4.837512969970703125e-4)
    rest = rest - turns * F32(7.54978995489188216e-8)
    sq = rest * rest
    sine = rest + rest * sq * (
        F32(-1.6666654611e-1) + sq * (F32(8.3321608736e-3) + sq * F32(-1.9515295891e-4))
    )
    cosine = (
        1.0
        - 0.5 * sq
        + sq * sq * (F32(4.166664568298827e-2) + sq * (F32(-1.388731625493765e-3) + sq * F32(2.443315711809948e-5)))
    )
    quarter = turns.astype(jnp.int32)
    odd = (quarter & 1) == 1
    flip = (quarter & 2) == 2
    base_s = jnp.where(odd, cosine, sine)
    base_c = jnp.where(odd, -sine, cosine)
    return jnp.where(flip, -base_s, base_s), jnp.where(flip, -base_c, base_c)


def rotary_tables(pos, freqs):
    sine, cosine = sin_cos(pos * freqs)
    lane = lax.broadcasted_iota(jnp.int32, sine.shape, 1)
    return cosine, jnp.where(lane < HALF, -sine, sine)


def swap(rows):
    return pltpu.roll(rows, HALF, 1)


def unit(rows):
    scale = lax.rsqrt(jnp.sum(rows * rows, axis=-1, keepdims=True) * (1.0 / DH) + EPS)
    return rows * scale, scale


def turn(unit_rows, gain, cosine, sine):
    scaled = unit_rows * gain
    return (scaled * cosine + swap(scaled) * sine).astype(BF)


def turn_back(grad, cosine, sine):
    return grad * cosine - swap(grad) * sine


def norm_back(scaled_grad, unit_rows, scale, gain):
    inner = scaled_grad * gain
    mean = jnp.sum(inner * unit_rows, axis=-1, keepdims=True) * (1.0 / DH)
    return scale * (inner - unit_rows * mean)


def low_rows(shape):
    return (lax.broadcasted_iota(jnp.int32, shape, 0) & 7) < 4


def part_rows(both):
    left, right = both[:DH], both[DH:]
    low = low_rows(left.shape)
    one = jnp.where(low, left, pltpu.roll(right, 4, 0))
    two = jnp.where(low, pltpu.roll(left, DH - 4, 0), right)
    return one, two


def join_rows(one, two):
    low = low_rows(one.shape)
    left = jnp.where(low, one, pltpu.roll(two, 4, 0))
    right = jnp.where(low, pltpu.roll(one, DH - 4, 0), two)
    return left, right


def audio_index():
    row = lax.broadcasted_iota(jnp.int32, (DH, DH), 0)
    inside = row & 7
    return jnp.where(inside < 4, 0, 60) + (row >> 3) * 4 + inside


def dot_nt(a, b):
    return lax.dot_general(a, b, (((1,), (1,)), ((), ())), preferred_element_type=F32)


def dot_tn(a, b):
    return lax.dot_general(a, b, (((0,), (0,)), ((), ())), preferred_element_type=F32)


def dot_nn(a, b):
    return lax.dot_general(a, b, (((1,), (0,)), ((), ())), preferred_element_type=F32)


def lanes(head):
    return pl.ds(pl.multiple_of(head * DH, DH), DH)


def heads_of(core):
    return core * HALF_HEADS


def fetch(pairs, done):
    copies = [pltpu.make_async_copy(far, near, done.at[at]) for at, (far, near) in enumerate(pairs)]
    for copy in copies:
        copy.start()
    return copies


def finish(copies):
    for copy in copies:
        copy.wait()


def spread_tile(out, at, rows):
    out[:, at] = jnp.broadcast_to(rows.astype(BF)[None], (32, 8, DH))


def payload_kernel(apos_far, aq_far, ac_far, ak_far, av_far, out, apos, aq, ac, ak, av, done):
    finish(fetch(((aq_far, aq), (ac_far, ac), (ak_far, ak), (av_far, av), (apos_far, apos)), done))
    base = heads_of(lax.axis_index("aseq"))
    for j in range(HALF_HEADS):
        columns = lanes(base + j)
        for at, pair in enumerate(((aq, ac), (ak, av))):
            spread_tile(out, 2 * j + at, jnp.concatenate([ref[0, :, columns].astype(F32) for ref in pair], axis=0))
    inside = lax.broadcasted_iota(jnp.int32, (8, DH), 0) & 3
    lane = lax.broadcasted_iota(jnp.int32, (8, DH), 1)
    pos = own_places(apos, inside)
    spread_tile(out, 2 * HALF_HEADS, jnp.where(lane < HALF, pos >> 6, pos & 63).astype(F32))


def own_places(apos, inside):
    early = jnp.where(inside == 0, apos[0, 0], apos[0, 1])
    late = jnp.where(inside == 2, apos[0, 2], apos[0, 3])
    return jnp.where(inside < 2, early, late)


def send_kernel(vq, vk, vv, vc, vpos, out):
    columns = pl.ds(pl.multiple_of(heads_of(1 - lax.axis_index("aseq")) * DH, DH), WIDTH)
    for at, ref in enumerate((vq, vk, vv, vc)):
        out[at * DH : (at + 1) * DH] = ref[:, columns]
    row = lax.broadcasted_iota(jnp.int32, (16, DH), 0)
    pos = jnp.broadcast_to(vpos[...], (16, DH))
    places = jnp.where(row == 0, pos >> 6, pos & 63).astype(F32).astype(BF)
    out[4 * DH : 4 * DH + 16] = jnp.concatenate([places] * HALF_HEADS, axis=1)


def video_mask(vlen, core):
    place = lax.axis_index("vseq") * 2 + core
    row = lax.broadcasted_iota(jnp.int32, (DH, DH), 0)
    return [(row + where * DH < vlen[0]).astype(F32) for where in (place, place + 1 - 2 * core)]


def video_kernel(
    vlen, vq, vk, vv, vc, got, pos_own, freqs, gains,
    keys, queries_far, keys_far, raw_vk_far, unit_vk_far, tables_far,
    queries, raw_vk, unit_vk, tables, done,
):
    core = lax.axis_index("aseq")
    base = heads_of(core)
    masks = video_mask(vlen, core)
    places = got[4 * DH : 4 * DH + 16, 0:DH].astype(F32)
    for at, pos in enumerate((pos_own[...].astype(F32), places[0:1] * 64.0 + places[1:2])):
        rows = slice(at * DH, (at + 1) * DH)
        spread = jnp.transpose(jnp.broadcast_to(pos, (DH, DH)))
        tables[0, rows], tables[1, rows] = rotary_tables(spread, freqs[...])
        tables[2, rows] = masks[at]

    def one_head(j, carry):
        columns = lanes(j)
        own_columns = lanes(base + j)
        for at in range(2):
            rows = slice(at * DH, (at + 1) * DH)
            take = (lambda ref, index: ref[:, own_columns]) if at == 0 else (lambda ref, index: got[index * DH : (index + 1) * DH, columns])
            cosine, sine, mask = tables[0, rows], tables[1, rows], tables[2, rows]
            query, key = take(vq, 0), take(vk, 1)
            queries[j, 0, rows] = query
            raw_vk[j, rows] = key
            keys[j, 1, rows] = take(vv, 2)
            queries[j, 2, rows] = (take(vc, 3).astype(F32) * mask).astype(BF)
            unit_query, _ = unit(query.astype(F32))
            unit_key, _ = unit(key.astype(F32))
            queries[j, 1, rows] = turn(unit_query, gains[pl.ds(base + j, 1), :], cosine, sine)
            keys[j, 0, rows] = turn(unit_key, gains[pl.ds(H + base + j, 1), :], cosine, sine)
            unit_vk[j, rows] = unit_key
        return carry

    lax.fori_loop(0, HALF_HEADS, one_head, 0)
    finish(
        fetch(
            (
                (queries, queries_far), (keys, keys_far), (raw_vk, raw_vk_far), (unit_vk, unit_vk_far),
                (tables, tables_far),
            ),
            done,
        )
    )


def audio_tables(gathered, freqs, alen):
    lane = lax.broadcasted_iota(jnp.int32, (DH, DH), 1)
    apos, _ = part_rows(gathered[:, 2 * HALF_HEADS].astype(F32).reshape(2 * DH, DH))
    apos = jnp.where(lane < HALF, apos * 64.0, apos)
    apos = apos + swap(apos)
    cosine, sine = rotary_tables(apos, freqs[...])
    return cosine, sine, (audio_index() < alen[0]).astype(F32)


def scores_kernel(alen, vlen, gathered, keys, freqs, gains, sums, gathered_far, tables, mask, done):
    copies = fetch([(gathered, gathered_far)], done)
    core = lax.axis_index("aseq")
    base = heads_of(core)
    tables[0], tables[1], tables[2] = audio_tables(gathered, freqs, alen)
    mask[0:DH], mask[DH : 2 * DH] = video_mask(vlen, core)
    found = []
    for j in range(HALF_HEADS):
        aq, ac = part_rows(gathered[:, 2 * j].astype(F32).reshape(2 * DH, DH))
        rows, _ = unit(aq)
        query = turn(rows, gains[pl.ds(2 * H + base + j, 1), :], tables[0], tables[1])
        cross = jnp.exp(dot_nt(keys[j, 0], query) * SCALE) * mask[...]
        dprob = dot_nt(keys[j, 1], (ac * tables[2]).astype(BF))
        found.append((jnp.sum(cross, axis=0, keepdims=True), jnp.sum(cross * dprob, axis=0, keepdims=True)))
    rows = [pair[0] for pair in found] + [pair[1] for pair in found]
    for at in range(3):
        block = jnp.concatenate(rows[4 * at : 4 * at + 4], axis=0)
        sums[:, at] = jnp.broadcast_to(block[None], (32, 4, DH))
    finish(copies)


EXPO, DPROB, UNIT_AQ, UNIT_VK, HEAD_ROWS = 0, 2 * DH, 4 * DH, 5 * DH, 7 * DH
TABLES = HALF_HEADS * HEAD_ROWS
COS_V, SIN_V, COS_A, SIN_A, GAINS = TABLES, TABLES + 256, TABLES + 512, TABLES + 640, TABLES + 768
GAIN_VK, GAIN_AQ, GAIN_SUMS, ALL_ROWS = GAINS, GAINS + 8, GAINS + 16, GAINS + 40


def rows_of(j, start, count):
    return pl.ds(pl.multiple_of(j * HEAD_ROWS + start, DH), count)


def queries_kernel(
    alen, vlen, queries_far, keys_far, unit_vk_far, video_far, gathered_far, freqs, gains,
    shared, part_far, grad_far, audio_far,
    queries, keys, gathered, masks, part, grads, audio, done_in, done_step, done_out,
):
    def coming(step):
        heads, rows = pl.ds(2 * step, 2), pl.ds(4 * step, 4)
        pairs = (
            (gathered_far.at[:, rows], gathered.at[:, rows]),
            (keys_far.at[heads], keys.at[heads]),
            (queries_far.at[heads], queries.at[heads]),
        )
        return [pltpu.make_async_copy(far, near, done_step.at[step, at]) for at, (far, near) in enumerate(pairs)]

    places = 2 * HALF_HEADS
    tables = fetch(
        [
            (gathered_far.at[:, places : places + 1], gathered.at[:, places : places + 1]),
            (video_far.at[0 : 2 * 2 * DH], shared.at[COS_V : COS_V + 4 * DH]),
        ],
        done_in,
    )
    for step in range(3):
        for copy in coming(step):
            copy.start()
    units = fetch(
        [(unit_vk_far.at[j], shared.at[j * HEAD_ROWS + UNIT_VK : (j + 1) * HEAD_ROWS]) for j in range(HALF_HEADS)],
        done_in.at[2 : 2 + HALF_HEADS],
    )
    core = lax.axis_index("aseq")
    base = heads_of(core)
    masks[DH : 2 * DH], masks[2 * DH : 3 * DH] = video_mask(vlen, core)
    shared[GAINS:ALL_ROWS] = jnp.zeros((ALL_ROWS - GAINS, DH), F32)
    tables[0].wait()
    shared[COS_A:SIN_A], shared[SIN_A:GAINS], masks[0:DH] = audio_tables(gathered, freqs, alen)
    tables[1].wait()

    def one_head(j):
        cos_v, sin_v, mask_v = shared[COS_V:SIN_V], shared[SIN_V:COS_A], masks[DH : 3 * DH]
        cos_a, sin_a, mask_a = shared[COS_A:SIN_A], shared[SIN_A:GAINS], masks[0:DH]
        gain_aq = gains[pl.ds(2 * H + base + j, 1), :]
        shared[pl.ds(GAIN_VK + j, 1), :] = gains[pl.ds(H + base + j, 1), :]
        shared[pl.ds(GAIN_AQ + j, 1), :] = gain_aq
        aq, ac = part_rows(gathered[:, 2 * j].astype(F32).reshape(2 * DH, DH))
        ak, av = part_rows(gathered[:, 2 * j + 1].astype(F32).reshape(2 * DH, DH))
        av = av.astype(BF)
        ac = (ac * mask_a).astype(BF)
        unit_aq, _ = unit(aq)
        low_aq = turn(unit_aq, gain_aq, cos_a, sin_a)
        unit_ak, _ = unit(ak)
        low_ak = turn(unit_ak, gains[pl.ds(3 * H + base + j, 1), :], cos_a, sin_a)
        shared[rows_of(j, EXPO, 2 * DH), :] = jnp.exp(dot_nt(keys[j, 0], low_aq) * SCALE) * mask_v
        shared[rows_of(j, DPROB, 2 * DH), :] = dot_nt(keys[j, 1], ac)
        shared[rows_of(j, UNIT_AQ, DH), :] = unit_aq
        audio[j, 0] = low_aq
        audio[j, 1] = ac
        rows, cots = queries[j, 1], queries[j, 2]
        expd = jnp.exp(dot_nt(low_ak, rows) * SCALE) * jnp.concatenate([mask_a, mask_a], axis=1)
        prob = expd * (1.0 / jnp.sum(expd, axis=0, keepdims=True))
        dp = dot_nt(av, cots)
        delta = jnp.sum(prob * dp, axis=0, keepdims=True)
        dscore = (prob * (dp - delta)).astype(BF)
        dk = dot_nn(dscore, rows) * SCALE
        dv = dot_nn(prob.astype(BF), cots)
        back = turn_back(dot_tn(dscore, low_ak) * SCALE, cos_v, sin_v)
        unit_vq, scale_vq = unit(queries[j, 0].astype(F32))
        grads[j] = norm_back(back, unit_vq, scale_vq, gains[pl.ds(base + j, 1), :]).astype(BF)
        shared[pl.ds(GAIN_SUMS + j, 1), :] = jnp.sum(back * unit_vq, axis=0, keepdims=True)
        sum_ak = jnp.sum(turn_back(dk, cos_a, sin_a) * unit_ak, axis=0, keepdims=True)
        shared[pl.ds(GAIN_SUMS + 18 + j, 1), :] = sum_ak
        return dk, dv

    def going(step):
        heads = pl.ds(2 * step, 2)
        tiles = [(part.at[:, at + step], part_far.at[:, at + step]) for at in (0, 3)]
        pairs = tiles + [(grads.at[heads], grad_far.at[heads]), (audio.at[heads], audio_far.at[heads])]
        return [pltpu.make_async_copy(near, far, done_out.at[step, at]) for at, (near, far) in enumerate(pairs)]

    def pair(step, carry):
        finish(coming(step))
        found = [one_head(2 * step + e) for e in range(2)]
        for array in range(2):
            left, right = join_rows(found[0][array], found[1][array])
            part[0:16, array * 3 + step] = left.reshape(16, 8, DH).astype(BF)
            part[16:32, array * 3 + step] = right.reshape(16, 8, DH).astype(BF)
        for copy in going(step):
            copy.start()
        return carry

    lax.fori_loop(0, 3, pair, 0)
    finish(units)
    for step in range(3):
        finish(going(step))


def back_kernel(part_far, totals, shared, merged_far, merged, gain_rows, done):
    coming = fetch([(part_far, merged.at[:, 3:9])], done)
    copies = []
    gain_rows[...] = shared[GAIN_SUMS:ALL_ROWS]
    blocks = [jnp.sum(totals[:, at], axis=0) for at in range(3)]
    rows = [blocks[r // 4][r % 4 : r % 4 + 1] for r in range(2 * HALF_HEADS)]
    found = []
    for j in range(HALF_HEADS):
        start = j * HEAD_ROWS
        cos_v, sin_v = shared[COS_V:SIN_V], shared[SIN_V:COS_A]
        cos_a, sin_a = shared[COS_A:SIN_A], shared[SIN_A:GAINS]
        inverse = 1.0 / rows[j]
        delta = rows[HALF_HEADS + j] * inverse
        prob = shared[start + EXPO : start + DPROB] * inverse
        dscore = (prob * (shared[start + DPROB : start + UNIT_AQ] - delta)).astype(BF)
        unit_aq, unit_vk = shared[start + UNIT_AQ : start + UNIT_VK], shared[start + UNIT_VK : start + HEAD_ROWS]
        low_vk = turn(unit_vk, shared[GAIN_VK + j : GAIN_VK + j + 1], cos_v, sin_v)
        low_aq = turn(unit_aq, shared[GAIN_AQ + j : GAIN_AQ + j + 1], cos_a, sin_a)
        dq = dot_tn(dscore, low_vk) * SCALE
        dk = dot_nn(dscore, low_aq) * SCALE
        back = turn_back(dk, cos_v, sin_v)
        gain_rows[6 + j : 7 + j, :] = jnp.sum(back * unit_vk, axis=0, keepdims=True)
        back = turn_back(dq, cos_a, sin_a)
        gain_rows[12 + j : 13 + j, :] = jnp.sum(back * unit_aq, axis=0, keepdims=True)
        found.append(dq)
        if j % 2 == 1:
            left, right = join_rows(found[j - 1], found[j])
            merged[0:16, j // 2] = left.reshape(16, 8, DH).astype(BF)
            merged[16:32, j // 2] = right.reshape(16, 8, DH).astype(BF)
            if j == HALF_HEADS - 1:
                finish(coming)
                copies += fetch([(merged.at[:, 0:9], merged_far.at[:, 0:9])], done.at[1:2])
    for at in range(3):
        spread_tile(merged, 9 + at, gain_rows[8 * at : 8 * at + 8, :])
    copies += fetch([(merged.at[:, 9:12], merged_far.at[:, 9:12])], done.at[2:3])
    finish(copies)


def keys_kernel(
    vlen, raw_vk_far, keys_far, video_far, grad_far, audio_far, totals, gains,
    key_own, value_own, other, raw_vk, keys, tables, audio, mask, sums, done,
):
    copies = fetch(
        (
            (raw_vk_far, raw_vk), (keys_far, keys), (video_far.at[0 : 2 * 2 * DH], tables), (audio_far, audio),
            (grad_far.at[:, DH : 2 * DH], other.at[0]),
        ),
        done,
    )
    core = lax.axis_index("aseq")
    base = heads_of(core)
    mask[0:DH], mask[DH : 2 * DH] = video_mask(vlen, core)
    for at in range(3):
        sums[4 * at : 4 * at + 4, :] = jnp.sum(totals[:, at], axis=0)
    finish(copies)

    def one_head(j, carry):
        cos_v, sin_v = tables[0 : 2 * DH], tables[2 * DH : 4 * DH]
        inverse = 1.0 / sums[pl.ds(j, 1), :]
        delta = sums[pl.ds(HALF_HEADS + j, 1), :] * inverse
        expo = jnp.exp(dot_nt(keys[j, 0], audio[j, 0]) * SCALE) * mask[...]
        prob = expo * inverse
        dscore = (prob * (dot_nt(keys[j, 1], audio[j, 1]) - delta)).astype(BF)
        dk = dot_nn(dscore, audio[j, 0]) * SCALE
        dv = dot_nn(prob.astype(BF), audio[j, 1]).astype(BF)
        unit_vk, scale_vk = unit(raw_vk[j].astype(F32))
        grad = norm_back(turn_back(dk, cos_v, sin_v), unit_vk, scale_vk, gains[pl.ds(H + base + j, 1), :]).astype(BF)
        key_own[j], value_own[j] = grad[:DH], dv[:DH]
        other[1, j], other[2, j] = grad[DH:], dv[DH:]
        return carry

    lax.fori_loop(0, HALF_HEADS, one_head, 0)


def place_kernel(query_own, key_own, value_own, got, grad_vq, grad_vk, grad_vv):
    core = lax.axis_index("aseq")
    for j in range(HALF_HEADS):
        own, other = lanes(heads_of(core) + j), lanes(heads_of(1 - core) + j)
        for at, (mine, grad) in enumerate(((query_own, grad_vq), (key_own, grad_vk), (value_own, grad_vv))):
            grad[:, own] = mine[j, 0:DH]
            grad[:, other] = got[at, j]


def add_peers(got):
    total = got[0].astype(F32)
    for v in range(1, 32):
        total = total + got[v].astype(F32)
    return total


def audio_kernel(
    apos_far, aq_far, ak_far, freqs_far, gains_far, after, got, out, gain_out, apos, aq, ak, freqs, gains, done
):
    copies = fetch(((apos_far, apos), (aq_far, aq), (ak_far, ak), (freqs_far, freqs), (gains_far, gains)), done)
    base = heads_of(lax.axis_index("aseq"))
    acc = add_peers(got)
    gain_out[...] = jnp.broadcast_to(acc[9:12].reshape(1, 24, DH), gain_out.shape)
    finish(copies)
    pos = own_places(apos, lax.broadcasted_iota(jnp.int32, (8, DH), 0) & 3)
    cosine, sine = rotary_tables(pos.astype(F32), freqs[...])
    low = low_rows((8, DH))

    def rows_back(ref, gain_at, grad, at):
        first = base + 2 * at
        rows = jnp.concatenate([ref[0, :, lanes(first + e)].astype(F32) for e in range(2)], axis=0)
        gain = jnp.where(low, gains[pl.ds(gain_at * H + first, 1), :], gains[pl.ds(gain_at * H + first + 1, 1), :])
        unit_rows, scale = unit(rows)
        return norm_back(turn_back(grad, cosine, sine), unit_rows, scale, gain)

    for at in range(3):
        dq = rows_back(aq, 2, acc[at], at)
        dk = rows_back(ak, 3, acc[3 + at], at)
        dv = acc[6 + at]
        left = jnp.where(low, dq, pltpu.roll(dk, 4, 0))
        right = jnp.where(low, pltpu.roll(dq, 4, 0), dk)
        out[:, 2 * at * DH : (2 * at + 1) * DH] = jnp.concatenate([left, dv], axis=0).astype(BF)
        out[:, (2 * at + 1) * DH : (2 * at + 2) * DH] = jnp.concatenate([right, pltpu.roll(dv, 4, 0)], axis=0).astype(BF)


def last_kernel(own, other, gains, grad_aq, grad_ak, grad_av, sum_vq, sum_vk, sum_aq, sum_ak):
    front = lax.axis_index("aseq") == 0
    mine, others = own[...].astype(F32), other[...].astype(F32)
    for at, value in enumerate((jnp.where(front, mine, others), jnp.where(front, others, mine))):
        columns = slice(at * WIDTH, (at + 1) * WIDTH)
        grad_aq[:, columns] = value[0:4].astype(BF)
        grad_ak[:, columns] = value[4:8].astype(BF)
        grad_av[:, columns] = value[8:12].astype(BF)
    for half in range(2):
        total = gains[half]
        for d in range(1, gains.shape[0] // 2):
            total = total + gains[2 * d + half]
        for at, ref in enumerate((sum_vq, sum_vk, sum_aq, sum_ak)):
            ref[6 * half : 6 * half + 6, :] = total[6 * at : 6 * at + 6]


NEAR, FAR = pltpu.VMEM, pltpu.HBM


def call(kernel, name, outs, ins, smem=0, far=0, scratch=()):
    def shape_of(shape, dtype, space=None):
        return jax.ShapeDtypeStruct(shape, dtype) if space is None else space(shape, dtype)

    ins = [pltpu.with_memory_space_constraint(x, FAR) if smem <= at < smem + far else x for at, x in enumerate(ins)]
    return pl.pallas_call(
        kernel,
        name=name,
        out_shape=[shape_of(*out) for out in outs],
        in_specs=[pl.BlockSpec(memory_space=pltpu.SMEM)] * smem
        + [pl.BlockSpec(memory_space=FAR)] * far
        + [pl.BlockSpec(memory_space=NEAR)] * (len(ins) - smem - far),
        out_specs=[pl.BlockSpec(memory_space=FAR if FAR in out else NEAR) for out in outs],
        scratch_shapes=list(scratch),
        compiler_params=pltpu.CompilerParams(vmem_limit_bytes=VMEM_LIMIT),
    )(*ins)


def local(
    video_query, video_key, video_value, video_grad,
    audio_query, audio_key, audio_value, audio_grad,
    video_pos, audio_pos, video_len, audio_len,
    gain_vq, gain_vk, gain_aq, gain_ak,
):
    F = H * DH
    groups = lax.axis_size("vseq")
    clips = lax.axis_size("dp")
    exchange = functools.partial(lax.ppermute, axis_name="aseq", perm=[(0, 1), (1, 0)])
    to_group = functools.partial(lax.all_to_all, axis_name="vseq", split_axis=0, concat_axis=0, tiled=True)
    freqs = frequencies()
    gains = jnp.concatenate([gain_vq, gain_vk, gain_aq, gain_ak]).reshape(4 * H, DH)
    video = [video_query[0], video_key[0], video_value[0], video_grad[0]]
    half = (HALF_HEADS, DH, DH)
    tiles = (groups, 2 * HALF_HEADS, 8, DH)
    six = (HALF_HEADS, 2 * DH, DH)
    queries_shape, keys_shape = (HALF_HEADS, 3, 2 * DH, DH), (HALF_HEADS, 2, 2 * DH, DH)
    own_rows = pltpu.VMEM((1, 4, F), BF)
    places = pltpu.SMEM((1, 4), jnp.int32)
    dmas = lambda count: pltpu.SemaphoreType.DMA((count,))

    (payload,) = call(
        payload_kernel,
        "payload",
        [((groups, 2 * HALF_HEADS + 1, 8, DH), BF)],
        [audio_pos, audio_query, audio_grad, audio_key, audio_value],
        far=5,
        scratch=[places] + [own_rows] * 4 + [dmas(5)],
    )
    gathered = to_group(payload)

    (send,) = call(send_kernel, "send", [((4 * DH + 16, WIDTH), BF)], [*video, video_pos])
    video_got = exchange(send)
    keys_near, queries, keys, raw_vk, unit_vk, video_tables = call(
        video_kernel,
        "video",
        [
            (keys_shape, BF, NEAR), (queries_shape, BF, FAR), (keys_shape, BF, FAR), (six, BF, FAR), (six, F32, FAR),
            ((3, 2 * DH, DH), F32, FAR),
        ],
        [video_len, *video, video_got, video_pos, freqs, gains],
        smem=1,
        scratch=[
            pltpu.VMEM(queries_shape, BF), pltpu.VMEM(six, BF), pltpu.VMEM(six, F32),
            pltpu.VMEM((3, 2 * DH, DH), F32), dmas(5),
        ],
    )

    gathered_shape = (groups, 2 * HALF_HEADS + 1, 8, DH)
    sums, gathered = call(
        scores_kernel,
        "scores",
        [((groups, 3, 4, DH), F32), (gathered_shape, BF, FAR)],
        [audio_len, video_len, gathered, keys_near, freqs, gains],
        smem=2,
        scratch=[pltpu.VMEM((3, DH, DH), F32), pltpu.VMEM((2 * DH, DH), F32), dmas(1)],
    )
    totals = to_group(sums)

    video_tables = video_tables.reshape(6 * DH, DH)
    part_shape, audio_shape = (groups, 6, 8, DH), (HALF_HEADS, 2, DH, DH)
    shared, part, query_grad, audio = call(
        queries_kernel,
        "queries",
        [((ALL_ROWS, DH), F32, NEAR), (part_shape, BF, FAR), (six, BF, FAR), (audio_shape, BF, FAR)],
        [audio_len, video_len, queries, keys, unit_vk, video_tables, gathered, freqs, gains],
        smem=2,
        far=5,
        scratch=[
            pltpu.VMEM(queries_shape, BF), pltpu.VMEM(keys_shape, BF), pltpu.VMEM(gathered_shape, BF),
            pltpu.VMEM((3 * DH, DH), F32), pltpu.VMEM(part_shape, BF), pltpu.VMEM(six, BF),
            pltpu.VMEM(audio_shape, BF), dmas(2 + HALF_HEADS), pltpu.SemaphoreType.DMA((3, 3)), pltpu.SemaphoreType.DMA((3, 4)),
        ],
    )

    (merged,) = call(
        back_kernel,
        "back",
        [(tiles, BF, FAR)],
        [part, totals, shared],
        far=1,
        scratch=[pltpu.VMEM(tiles, BF), pltpu.VMEM((24, DH), F32), dmas(3)],
    )
    got = to_group(merged)

    key_own, value_own, other = call(
        keys_kernel,
        "keys",
        [(half, BF), (half, BF), ((3, *half), BF)],
        [video_len, raw_vk, keys, video_tables, query_grad, audio, totals, gains],
        smem=1,
        far=5,
        scratch=[
            pltpu.VMEM(six, BF), pltpu.VMEM(keys_shape, BF), pltpu.VMEM((4 * DH, DH), F32),
            pltpu.VMEM(audio_shape, BF), pltpu.VMEM((2 * DH, DH), F32), pltpu.VMEM((16, DH), F32), dmas(5),
        ],
    )
    other_got = exchange(other)
    grad_vq, grad_vk, grad_vv = call(
        place_kernel, "place", [((DH, F), BF)] * 3, [query_grad, key_own, value_own, other_got]
    )

    audio_half, gain_rows = call(
        audio_kernel,
        "audio",
        [((16, WIDTH), BF), ((2 * clips, 24, DH), F32)],
        [audio_pos, audio_query, audio_key, freqs, gains, grad_vv, got],
        far=6,
        scratch=[places, own_rows, own_rows, pltpu.VMEM((1, DH), F32), pltpu.VMEM((4 * H, DH), F32), dmas(5)],
    )
    gain_got = lax.all_to_all(gain_rows, ("dp", "aseq"), 0, 0, tiled=True)
    audio_got = exchange(audio_half)
    grad_aq, grad_ak, grad_av, sum_vq, sum_vk, sum_aq, sum_ak = call(
        last_kernel,
        "last",
        [((4, F), BF)] * 3 + [((H, DH), F32)] * 4,
        [audio_half, audio_got, gain_got],
    )
    return (
        grad_vq[None],
        grad_vk[None],
        grad_vv[None],
        grad_aq[None],
        grad_ak[None],
        grad_av[None],
        sum_vq.reshape(F),
        sum_vk.reshape(F),
        sum_aq.reshape(F),
        sum_ak.reshape(F),
    )


def solution(mesh):
    video = P("dp", ("vseq", "aseq"), None)
    audio = P("dp", "vseq", None)
    in_specs = (
        (video,) * 4
        + (audio,) * 4
        + (P("dp", ("vseq", "aseq")), P("dp", "vseq"), P("dp"), P("dp"))
        + (P(),) * 4
    )
    out_specs = (video,) * 3 + (audio,) * 3 + (P(),) * 4
    return jax.shard_map(local, mesh=mesh, in_specs=in_specs, out_specs=out_specs, check_vma=False)
```

```python
import functools

import jax
import jax.numpy as jnp
import numpy as np
from jax import lax
from jax.experimental import pallas as pl
from jax.experimental.pallas import tpu as pltpu
from jax.sharding import PartitionSpec as P

H = 12
DH = 128
HALF = DH // 2
EPS = 1e-06
THETA = 10000.0
SCALE = DH ** (-0.5)
BF = jnp.bfloat16
F32 = jnp.float32
VMEM_LIMIT = 24 * 1024 * 1024
HALF_HEADS = H // 2
WIDTH = HALF_HEADS * DH


def frequencies():
    freqs = np.power(np.float64(THETA), -(np.arange(HALF, dtype=np.float64) / HALF))
    return jnp.asarray(np.tile(freqs.astype(np.float32), 2).reshape(1, DH))


def sin_cos(angles):
    turns = jnp.floor(angles * F32(2.0 / np.pi) + 0.5)
    rest = angles - turns * F32(1.5703125)
    rest = rest - turns * F32(4.837512969970703125e-4)
    rest = rest - turns * F32(7.54978995489188216e-8)
    sq = rest * rest
    sine = rest + rest * sq * (
        F32(-1.6666654611e-1) + sq * (F32(8.3321608736e-3) + sq * F32(-1.9515295891e-4))
    )
    cosine = (
        1.0
        - 0.5 * sq
        + sq * sq * (F32(4.166664568298827e-2) + sq * (F32(-1.388731625493765e-3) + sq * F32(2.443315711809948e-5)))
    )
    quarter = turns.astype(jnp.int32)
    odd = (quarter & 1) == 1
    flip = (quarter & 2) == 2
    base_s = jnp.where(odd, cosine, sine)
    base_c = jnp.where(odd, -sine, cosine)
    return jnp.where(flip, -base_s, base_s), jnp.where(flip, -base_c, base_c)


def rotary_tables(pos, freqs):
    sine, cosine = sin_cos(pos * freqs)
    lane = lax.broadcasted_iota(jnp.int32, sine.shape, 1)
    return cosine, jnp.where(lane < HALF, -sine, sine)


def swap(rows):
    return pltpu.roll(rows, HALF, 1)


def unit(rows):
    scale = lax.rsqrt(jnp.sum(rows * rows, axis=-1, keepdims=True) * (1.0 / DH) + EPS)
    return rows * scale, scale


def turn(unit_rows, gain, cosine, sine):
    scaled = unit_rows * gain
    return (scaled * cosine + swap(scaled) * sine).astype(BF)


def turn_back(grad, cosine, sine):
    return grad * cosine - swap(grad) * sine


def norm_back(scaled_grad, unit_rows, scale, gain):
    inner = scaled_grad * gain
    mean = jnp.sum(inner * unit_rows, axis=-1, keepdims=True) * (1.0 / DH)
    return scale * (inner - unit_rows * mean)


def low_rows(shape):
    return (lax.broadcasted_iota(jnp.int32, shape, 0) & 7) < 4


def part_rows(both):
    left, right = both[:DH], both[DH:]
    low = low_rows(left.shape)
    one = jnp.where(low, left, pltpu.roll(right, 4, 0))
    two = jnp.where(low, pltpu.roll(left, DH - 4, 0), right)
    return one, two


def join_rows(one, two):
    low = low_rows(one.shape)
    left = jnp.where(low, one, pltpu.roll(two, 4, 0))
    right = jnp.where(low, pltpu.roll(one, DH - 4, 0), two)
    return left, right


def audio_index():
    row = lax.broadcasted_iota(jnp.int32, (DH, DH), 0)
    inside = row & 7
    return jnp.where(inside < 4, 0, 60) + (row >> 3) * 4 + inside


def dot_nt(a, b):
    return lax.dot_general(a, b, (((1,), (1,)), ((), ())), preferred_element_type=F32)


def dot_tn(a, b):
    return lax.dot_general(a, b, (((0,), (0,)), ((), ())), preferred_element_type=F32)


def dot_nn(a, b):
    return lax.dot_general(a, b, (((1,), (0,)), ((), ())), preferred_element_type=F32)


def lanes(head):
    return pl.ds(pl.multiple_of(head * DH, DH), DH)


def heads_of(core):
    return core * HALF_HEADS


def side_by_side(steps):
    steps, results = list(steps), {}
    running = dict(enumerate(steps))
    while running:
        for at in list(running):
            try:
                next(running[at])
            except StopIteration as end:
                results[at] = end.value
                del running[at]
    return [results[at] for at in range(len(steps))]


def fetch(pairs, done):
    copies = [pltpu.make_async_copy(far, near, done.at[at]) for at, (far, near) in enumerate(pairs)]
    for copy in copies:
        copy.start()
    return copies


def finish(copies):
    for copy in copies:
        copy.wait()


def spread_tile(out, at, rows):
    out[:, at] = jnp.broadcast_to(rows.astype(BF)[None], (32, 8, DH))


def payload_kernel(apos_far, aq_far, ac_far, ak_far, av_far, out_far, out, apos, aq, ac, ak, av, done, sent):
    finish(fetch(((aq_far, aq), (ac_far, ac), (ak_far, ak), (av_far, av), (apos_far, apos)), done))
    base = heads_of(lax.axis_index("aseq"))
    inside = lax.broadcasted_iota(jnp.int32, (8, DH), 0) & 3
    lane = lax.broadcasted_iota(jnp.int32, (8, DH), 1)
    pos = own_places(apos, inside)
    spread_tile(out, 2 * HALF_HEADS, jnp.where(lane < HALF, pos >> 6, pos & 63).astype(F32))
    copies = []
    for j in range(HALF_HEADS):
        columns = lanes(base + j)
        for at, pair in enumerate(((aq, ac), (ak, av))):
            spread_tile(out, 2 * j + at, jnp.concatenate([ref[0, :, columns].astype(F32) for ref in pair], axis=0))
        if j % 2 == 1:
            tiles = slice(2 * j - 2, 2 * j + 2 + (j == HALF_HEADS - 1))
            copies += fetch([(out.at[:, tiles], out_far.at[:, tiles])], sent.at[j // 2 : j // 2 + 1])
    finish(copies)


def own_places(apos, inside):
    early = jnp.where(inside == 0, apos[0, 0], apos[0, 1])
    late = jnp.where(inside == 2, apos[0, 2], apos[0, 3])
    return jnp.where(inside < 2, early, late)


def send_kernel(vq, vk, vv, vc, vpos, out):
    columns = pl.ds(pl.multiple_of(heads_of(1 - lax.axis_index("aseq")) * DH, DH), WIDTH)
    for at, ref in enumerate((vq, vk, vv, vc)):
        out[at * DH : (at + 1) * DH] = ref[:, columns]
    row = lax.broadcasted_iota(jnp.int32, (16, DH), 0)
    pos = jnp.broadcast_to(vpos[...], (16, DH))
    places = jnp.where(row == 0, pos >> 6, pos & 63).astype(F32).astype(BF)
    out[4 * DH : 4 * DH + 16] = jnp.concatenate([places] * HALF_HEADS, axis=1)


def video_mask(vlen, core):
    place = lax.axis_index("vseq") * 2 + core
    row = lax.broadcasted_iota(jnp.int32, (DH, DH), 0)
    return [(row + where * DH < vlen[0]).astype(F32) for where in (place, place + 1 - 2 * core)]


def video_kernel(
    vlen, vq, vk, vv, vc, got, pos_own, freqs, gains,
    keys, queries_far, keys_far, raw_vk_far, unit_vk_far, tables_far,
    queries, raw_vk, unit_vk, tables, done,
):
    core = lax.axis_index("aseq")
    base = heads_of(core)
    masks = video_mask(vlen, core)
    places = got[4 * DH : 4 * DH + 16, 0:DH].astype(F32)
    for at, pos in enumerate((pos_own[...].astype(F32), places[0:1] * 64.0 + places[1:2])):
        rows = slice(at * DH, (at + 1) * DH)
        spread = jnp.transpose(jnp.broadcast_to(pos, (DH, DH)))
        tables[0, rows], tables[1, rows] = rotary_tables(spread, freqs[...])
        tables[2, rows] = masks[at]

    def one_head(j, carry):
        columns = lanes(j)
        own_columns = lanes(base + j)
        for at in range(2):
            rows = slice(at * DH, (at + 1) * DH)
            take = (lambda ref, index: ref[:, own_columns]) if at == 0 else (lambda ref, index: got[index * DH : (index + 1) * DH, columns])
            cosine, sine, mask = tables[0, rows], tables[1, rows], tables[2, rows]
            query, key = take(vq, 0), take(vk, 1)
            queries[j, 0, rows] = query
            raw_vk[j, rows] = key
            keys[j, 1, rows] = take(vv, 2)
            queries[j, 2, rows] = (take(vc, 3).astype(F32) * mask).astype(BF)
            unit_query, _ = unit(query.astype(F32))
            unit_key, _ = unit(key.astype(F32))
            queries[j, 1, rows] = turn(unit_query, gains[pl.ds(base + j, 1), :], cosine, sine)
            keys[j, 0, rows] = turn(unit_key, gains[pl.ds(H + base + j, 1), :], cosine, sine)
            unit_vk[j, rows] = unit_key
        return carry

    lax.fori_loop(0, HALF_HEADS, one_head, 0)
    finish(
        fetch(
            (
                (queries, queries_far), (keys, keys_far), (raw_vk, raw_vk_far), (unit_vk, unit_vk_far),
                (tables, tables_far),
            ),
            done,
        )
    )


def audio_tables(gathered, freqs, alen):
    lane = lax.broadcasted_iota(jnp.int32, (DH, DH), 1)
    apos, _ = part_rows(gathered[:, 2 * HALF_HEADS].astype(F32).reshape(2 * DH, DH))
    apos = jnp.where(lane < HALF, apos * 64.0, apos)
    apos = apos + swap(apos)
    cosine, sine = rotary_tables(apos, freqs[...])
    return cosine, sine, (audio_index() < alen[0]).astype(F32)


def scores_kernel(alen, vlen, gathered, keys, freqs, gains, sums, gathered_far, tables, mask, done):
    copies = fetch([(gathered, gathered_far)], done)
    core = lax.axis_index("aseq")
    base = heads_of(core)
    tables[0], tables[1], tables[2] = audio_tables(gathered, freqs, alen)
    mask[0:DH], mask[DH : 2 * DH] = video_mask(vlen, core)

    def one_head(j):
        aq, ac = part_rows(gathered[:, 2 * j].astype(F32).reshape(2 * DH, DH))
        ac = (ac * tables[2]).astype(BF)
        yield
        rows, _ = unit(aq)
        yield
        query = turn(rows, gains[pl.ds(2 * H + base + j, 1), :], tables[0], tables[1])
        yield
        cross = dot_nt(keys[j, 0], query)
        dprob = dot_nt(keys[j, 1], ac)
        yield
        cross = jnp.exp(cross * SCALE) * mask[...]
        yield
        return jnp.sum(cross, axis=0, keepdims=True), jnp.sum(cross * dprob, axis=0, keepdims=True)

    found = side_by_side(one_head(j) for j in range(HALF_HEADS))
    rows = [pair[0] for pair in found] + [pair[1] for pair in found]
    for at in range(3):
        block = jnp.concatenate(rows[4 * at : 4 * at + 4], axis=0)
        sums[:, at] = jnp.broadcast_to(block[None], (32, 4, DH))
    finish(copies)


EXPO, DPROB, UNIT_AQ, UNIT_VK, HEAD_ROWS = 0, 2 * DH, 4 * DH, 5 * DH, 7 * DH
TABLES = HALF_HEADS * HEAD_ROWS
COS_V, SIN_V, COS_A, SIN_A, GAINS = TABLES, TABLES + 256, TABLES + 512, TABLES + 640, TABLES + 768
GAIN_VK, GAIN_AQ, GAIN_SUMS, ALL_ROWS = GAINS, GAINS + 8, GAINS + 16, GAINS + 40


def rows_of(j, start, count):
    return pl.ds(pl.multiple_of(j * HEAD_ROWS + start, DH), count)


def queries_kernel(
    alen, vlen, queries_far, keys_far, unit_vk_far, video_far, gathered_far, freqs, gains,
    shared, part_far, grad_far, audio_far,
    queries, keys, gathered, masks, part, grads, audio, done_in, done_step, done_out,
):
    def coming(step):
        heads, rows = pl.ds(2 * step, 2), pl.ds(4 * step, 4)
        pairs = (
            (gathered_far.at[:, rows], gathered.at[:, rows]),
            (keys_far.at[heads], keys.at[heads]),
            (queries_far.at[heads], queries.at[heads]),
        )
        return [pltpu.make_async_copy(far, near, done_step.at[step, at]) for at, (far, near) in enumerate(pairs)]

    places = 2 * HALF_HEADS
    tables = fetch(
        [
            (gathered_far.at[:, places : places + 1], gathered.at[:, places : places + 1]),
            (video_far.at[0 : 2 * 2 * DH], shared.at[COS_V : COS_V + 4 * DH]),
        ],
        done_in,
    )
    for step in range(3):
        for copy in coming(step):
            copy.start()
    units = fetch(
        [(unit_vk_far.at[j], shared.at[j * HEAD_ROWS + UNIT_VK : (j + 1) * HEAD_ROWS]) for j in range(HALF_HEADS)],
        done_in.at[2 : 2 + HALF_HEADS],
    )
    core = lax.axis_index("aseq")
    base = heads_of(core)
    masks[DH : 2 * DH], masks[2 * DH : 3 * DH] = video_mask(vlen, core)
    shared[GAINS:ALL_ROWS] = jnp.zeros((ALL_ROWS - GAINS, DH), F32)
    tables[0].wait()
    shared[COS_A:SIN_A], shared[SIN_A:GAINS], masks[0:DH] = audio_tables(gathered, freqs, alen)
    tables[1].wait()

    def one_head(j):
        cos_v, sin_v, mask_v = shared[COS_V:SIN_V], shared[SIN_V:COS_A], masks[DH : 3 * DH]
        cos_a, sin_a, mask_a = shared[COS_A:SIN_A], shared[SIN_A:GAINS], masks[0:DH]
        gain_aq = gains[pl.ds(2 * H + base + j, 1), :]
        shared[pl.ds(GAIN_VK + j, 1), :] = gains[pl.ds(H + base + j, 1), :]
        shared[pl.ds(GAIN_AQ + j, 1), :] = gain_aq
        aq, ac = part_rows(gathered[:, 2 * j].astype(F32).reshape(2 * DH, DH))
        ak, av = part_rows(gathered[:, 2 * j + 1].astype(F32).reshape(2 * DH, DH))
        av = av.astype(BF)
        ac = (ac * mask_a).astype(BF)
        yield
        unit_ak, _ = unit(ak)
        unit_aq, _ = unit(aq)
        unit_vq, scale_vq = unit(queries[j, 0].astype(F32))
        yield
        low_ak = turn(unit_ak, gains[pl.ds(3 * H + base + j, 1), :], cos_a, sin_a)
        low_aq = turn(unit_aq, gain_aq, cos_a, sin_a)
        audio[j, 0] = low_aq
        audio[j, 1] = ac
        shared[rows_of(j, UNIT_AQ, DH), :] = unit_aq
        yield
        rows, cots = queries[j, 1], queries[j, 2]
        expd = dot_nt(low_ak, rows)
        dp = dot_nt(av, cots)
        yield
        expd = jnp.exp(expd * SCALE) * jnp.concatenate([mask_a, mask_a], axis=1)
        prob = expd * (1.0 / jnp.sum(expd, axis=0, keepdims=True))
        yield
        cross = dot_nt(keys[j, 0], low_aq)
        shared[rows_of(j, DPROB, 2 * DH), :] = dot_nt(keys[j, 1], ac)
        delta = jnp.sum(prob * dp, axis=0, keepdims=True)
        dscore = (prob * (dp - delta)).astype(BF)
        yield
        dq = dot_tn(dscore, low_ak)
        dk = dot_nn(dscore, rows)
        dv = dot_nn(prob.astype(BF), cots)
        yield
        shared[rows_of(j, EXPO, 2 * DH), :] = jnp.exp(cross * SCALE) * mask_v
        yield
        back = turn_back(dq * SCALE, cos_v, sin_v)
        dk = dk * SCALE
        shared[pl.ds(GAIN_SUMS + j, 1), :] = jnp.sum(back * unit_vq, axis=0, keepdims=True)
        yield
        grads[j] = norm_back(back, unit_vq, scale_vq, gains[pl.ds(base + j, 1), :]).astype(BF)
        yield
        sum_ak = jnp.sum(turn_back(dk, cos_a, sin_a) * unit_ak, axis=0, keepdims=True)
        shared[pl.ds(GAIN_SUMS + 18 + j, 1), :] = sum_ak
        return dk, dv

    def going(step):
        heads = pl.ds(2 * step, 2)
        tiles = [(part.at[:, at + step], part_far.at[:, at + step]) for at in (0, 3)]
        pairs = tiles + [(grads.at[heads], grad_far.at[heads]), (audio.at[heads], audio_far.at[heads])]
        return [pltpu.make_async_copy(near, far, done_out.at[step, at]) for at, (near, far) in enumerate(pairs)]

    def pair(step, carry):
        finish(coming(step))
        found = side_by_side(one_head(2 * step + e) for e in range(2))
        for array in range(2):
            left, right = join_rows(found[0][array], found[1][array])
            part[0:16, array * 3 + step] = left.reshape(16, 8, DH).astype(BF)
            part[16:32, array * 3 + step] = right.reshape(16, 8, DH).astype(BF)
        for copy in going(step):
            copy.start()
        return carry

    lax.fori_loop(0, 3, pair, 0)
    finish(units)
    for step in range(3):
        finish(going(step))


def back_kernel(part_far, totals, shared, merged_far, merged, gain_rows, done):
    coming = fetch([(part_far, merged.at[:, 3:9])], done)
    copies, found = [], []
    gain_rows[...] = shared[GAIN_SUMS:ALL_ROWS]
    blocks = [jnp.sum(totals[:, at], axis=0) for at in range(3)]
    rows = [blocks[r // 4][r % 4 : r % 4 + 1] for r in range(2 * HALF_HEADS)]

    def one_head(j):
        start = j * HEAD_ROWS
        cos_v, sin_v = shared[COS_V:SIN_V], shared[SIN_V:COS_A]
        cos_a, sin_a = shared[COS_A:SIN_A], shared[SIN_A:GAINS]
        unit_aq, unit_vk = shared[start + UNIT_AQ : start + UNIT_VK], shared[start + UNIT_VK : start + HEAD_ROWS]
        low_vk = turn(unit_vk, shared[GAIN_VK + j : GAIN_VK + j + 1], cos_v, sin_v)
        low_aq = turn(unit_aq, shared[GAIN_AQ + j : GAIN_AQ + j + 1], cos_a, sin_a)
        yield
        inverse = 1.0 / rows[j]
        delta = rows[HALF_HEADS + j] * inverse
        prob = shared[start + EXPO : start + DPROB] * inverse
        dscore = (prob * (shared[start + DPROB : start + UNIT_AQ] - delta)).astype(BF)
        yield
        dk = dot_nn(dscore, low_aq)
        dq = dot_tn(dscore, low_vk)
        yield
        back = turn_back(dk * SCALE, cos_v, sin_v)
        gain_rows[6 + j : 7 + j, :] = jnp.sum(back * unit_vk, axis=0, keepdims=True)
        yield
        dq = dq * SCALE
        back = turn_back(dq, cos_a, sin_a)
        gain_rows[12 + j : 13 + j, :] = jnp.sum(back * unit_aq, axis=0, keepdims=True)
        return dq

    for at in range(2):
        three = range(3 * at, 3 * at + 3)
        found += side_by_side(one_head(j) for j in three)
        for pair in ((0,), (1, 2))[at]:
            left, right = join_rows(found[2 * pair], found[2 * pair + 1])
            merged[0:16, pair] = left.reshape(16, 8, DH).astype(BF)
            merged[16:32, pair] = right.reshape(16, 8, DH).astype(BF)
    finish(coming)
    copies += fetch([(merged.at[:, 0:9], merged_far.at[:, 0:9])], done.at[1:2])
    for at in range(3):
        spread_tile(merged, 9 + at, gain_rows[8 * at : 8 * at + 8, :])
    copies += fetch([(merged.at[:, 9:12], merged_far.at[:, 9:12])], done.at[2:3])
    finish(copies)


def keys_kernel(
    vlen, raw_vk_far, keys_far, video_far, grad_far, audio_far, totals, gains,
    key_own, value_own, other, raw_vk, keys, tables, audio, mask, sums, done,
):
    copies = fetch(
        (
            (raw_vk_far, raw_vk), (keys_far, keys), (video_far.at[0 : 2 * 2 * DH], tables), (audio_far, audio),
            (grad_far.at[:, DH : 2 * DH], other.at[0]),
        ),
        done,
    )
    core = lax.axis_index("aseq")
    base = heads_of(core)
    mask[0:DH], mask[DH : 2 * DH] = video_mask(vlen, core)
    for at in range(3):
        sums[4 * at : 4 * at + 4, :] = jnp.sum(totals[:, at], axis=0)
    finish(copies)

    def one_head(j, carry):
        cos_v, sin_v = tables[0 : 2 * DH], tables[2 * DH : 4 * DH]
        inverse = 1.0 / sums[pl.ds(j, 1), :]
        delta = sums[pl.ds(HALF_HEADS + j, 1), :] * inverse
        expo = jnp.exp(dot_nt(keys[j, 0], audio[j, 0]) * SCALE) * mask[...]
        prob = expo * inverse
        dscore = (prob * (dot_nt(keys[j, 1], audio[j, 1]) - delta)).astype(BF)
        dk = dot_nn(dscore, audio[j, 0]) * SCALE
        dv = dot_nn(prob.astype(BF), audio[j, 1]).astype(BF)
        unit_vk, scale_vk = unit(raw_vk[j].astype(F32))
        grad = norm_back(turn_back(dk, cos_v, sin_v), unit_vk, scale_vk, gains[pl.ds(H + base + j, 1), :]).astype(BF)
        key_own[j], value_own[j] = grad[:DH], dv[:DH]
        other[1, j], other[2, j] = grad[DH:], dv[DH:]
        return carry

    lax.fori_loop(0, HALF_HEADS, one_head, 0)


def place_kernel(query_own, key_own, value_own, got, grad_vq, grad_vk, grad_vv):
    core = lax.axis_index("aseq")
    for j in range(HALF_HEADS):
        own, other = lanes(heads_of(core) + j), lanes(heads_of(1 - core) + j)
        for at, (mine, grad) in enumerate(((query_own, grad_vq), (key_own, grad_vk), (value_own, grad_vv))):
            grad[:, own] = mine[j, 0:DH]
            grad[:, other] = got[at, j]


def add_peers(got, tiles):
    total = got[0, tiles].astype(F32)
    for v in range(1, 32):
        total = total + got[v, tiles].astype(F32)
    return total


def audio_kernel(
    apos_far, aq_far, ak_far, freqs_far, gains_far, after, got, out, gain_far,
    apos, aq, ak, freqs, gains, gain_out, done,
):
    copies = fetch(((apos_far, apos), (aq_far, aq), (ak_far, ak), (freqs_far, freqs), (gains_far, gains)), done)
    base = heads_of(lax.axis_index("aseq"))
    acc = add_peers(got, slice(9, 12))
    gain_out[...] = jnp.broadcast_to(acc.reshape(1, 24, DH), gain_out.shape)
    sent = fetch([(gain_out, gain_far)], done.at[5:6])
    acc = add_peers(got, slice(0, 9))
    finish(copies)
    pos = own_places(apos, lax.broadcasted_iota(jnp.int32, (8, DH), 0) & 3)
    cosine, sine = rotary_tables(pos.astype(F32), freqs[...])
    low = low_rows((8, DH))

    def rows_back(ref, gain_at, grad, at):
        first = base + 2 * at
        rows = jnp.concatenate([ref[0, :, lanes(first + e)].astype(F32) for e in range(2)], axis=0)
        gain = jnp.where(low, gains[pl.ds(gain_at * H + first, 1), :], gains[pl.ds(gain_at * H + first + 1, 1), :])
        unit_rows, scale = unit(rows)
        return norm_back(turn_back(grad, cosine, sine), unit_rows, scale, gain)

    for at in range(3):
        dq = rows_back(aq, 2, acc[at], at)
        dk = rows_back(ak, 3, acc[3 + at], at)
        dv = acc[6 + at]
        left = jnp.where(low, dq, pltpu.roll(dk, 4, 0))
        right = jnp.where(low, pltpu.roll(dq, 4, 0), dk)
        out[:, 2 * at * DH : (2 * at + 1) * DH] = jnp.concatenate([left, dv], axis=0).astype(BF)
        out[:, (2 * at + 1) * DH : (2 * at + 2) * DH] = jnp.concatenate([right, pltpu.roll(dv, 4, 0)], axis=0).astype(BF)
    finish(sent)


def last_kernel(own, other, gains, grad_aq, grad_ak, grad_av, sum_vq, sum_vk, sum_aq, sum_ak):
    front = lax.axis_index("aseq") == 0
    mine, others = own[...].astype(F32), other[...].astype(F32)
    for at, value in enumerate((jnp.where(front, mine, others), jnp.where(front, others, mine))):
        columns = slice(at * WIDTH, (at + 1) * WIDTH)
        grad_aq[:, columns] = value[0:4].astype(BF)
        grad_ak[:, columns] = value[4:8].astype(BF)
        grad_av[:, columns] = value[8:12].astype(BF)
    for half in range(2):
        total = gains[half]
        for d in range(1, gains.shape[0] // 2):
            total = total + gains[2 * d + half]
        for at, ref in enumerate((sum_vq, sum_vk, sum_aq, sum_ak)):
            ref[6 * half : 6 * half + 6, :] = total[6 * at : 6 * at + 6]


NEAR, FAR = pltpu.VMEM, pltpu.HBM


def call(kernel, name, outs, ins, smem=0, far=0, scratch=()):
    def shape_of(shape, dtype, space=None):
        return jax.ShapeDtypeStruct(shape, dtype) if space is None else space(shape, dtype)

    ins = [pltpu.with_memory_space_constraint(x, FAR) if smem <= at < smem + far else x for at, x in enumerate(ins)]
    return pl.pallas_call(
        kernel,
        name=name,
        out_shape=[shape_of(*out) for out in outs],
        in_specs=[pl.BlockSpec(memory_space=pltpu.SMEM)] * smem
        + [pl.BlockSpec(memory_space=FAR)] * far
        + [pl.BlockSpec(memory_space=NEAR)] * (len(ins) - smem - far),
        out_specs=[pl.BlockSpec(memory_space=FAR if FAR in out else NEAR) for out in outs],
        scratch_shapes=list(scratch),
        compiler_params=pltpu.CompilerParams(vmem_limit_bytes=VMEM_LIMIT),
    )(*ins)


def local(
    video_query, video_key, video_value, video_grad,
    audio_query, audio_key, audio_value, audio_grad,
    video_pos, audio_pos, video_len, audio_len,
    gain_vq, gain_vk, gain_aq, gain_ak,
):
    F = H * DH
    groups = lax.axis_size("vseq")
    clips = lax.axis_size("dp")
    exchange = functools.partial(lax.ppermute, axis_name="aseq", perm=[(0, 1), (1, 0)])
    to_group = functools.partial(lax.all_to_all, axis_name="vseq", split_axis=0, concat_axis=0, tiled=True)
    freqs = frequencies()
    gains = jnp.concatenate([gain_vq, gain_vk, gain_aq, gain_ak]).reshape(4 * H, DH)
    video = [video_query[0], video_key[0], video_value[0], video_grad[0]]
    half = (HALF_HEADS, DH, DH)
    tiles = (groups, 2 * HALF_HEADS, 8, DH)
    six = (HALF_HEADS, 2 * DH, DH)
    queries_shape, keys_shape = (HALF_HEADS, 3, 2 * DH, DH), (HALF_HEADS, 2, 2 * DH, DH)
    gathered_shape = (groups, 2 * HALF_HEADS + 1, 8, DH)
    own_rows = pltpu.VMEM((1, 4, F), BF)
    places = pltpu.SMEM((1, 4), jnp.int32)
    dmas = lambda count: pltpu.SemaphoreType.DMA((count,))

    (payload,) = call(
        payload_kernel,
        "payload",
        [(gathered_shape, BF, FAR)],
        [audio_pos, audio_query, audio_grad, audio_key, audio_value],
        far=5,
        scratch=[pltpu.VMEM(gathered_shape, BF), places] + [own_rows] * 4 + [dmas(5), dmas(3)],
    )
    gathered = to_group(payload)

    (send,) = call(send_kernel, "send", [((4 * DH + 16, WIDTH), BF)], [*video, video_pos])
    video_got = exchange(send)
    keys_near, queries, keys, raw_vk, unit_vk, video_tables = call(
        video_kernel,
        "video",
        [
            (keys_shape, BF, NEAR), (queries_shape, BF, FAR), (keys_shape, BF, FAR), (six, BF, FAR), (six, F32, FAR),
            ((3, 2 * DH, DH), F32, FAR),
        ],
        [video_len, *video, video_got, video_pos, freqs, gains],
        smem=1,
        scratch=[
            pltpu.VMEM(queries_shape, BF), pltpu.VMEM(six, BF), pltpu.VMEM(six, F32),
            pltpu.VMEM((3, 2 * DH, DH), F32), dmas(5),
        ],
    )

    sums, gathered = call(
        scores_kernel,
        "scores",
        [((groups, 3, 4, DH), F32), (gathered_shape, BF, FAR)],
        [audio_len, video_len, gathered, keys_near, freqs, gains],
        smem=2,
        scratch=[pltpu.VMEM((3, DH, DH), F32), pltpu.VMEM((2 * DH, DH), F32), dmas(1)],
    )
    totals = to_group(sums)

    video_tables = video_tables.reshape(6 * DH, DH)
    part_shape, audio_shape = (groups, 6, 8, DH), (HALF_HEADS, 2, DH, DH)
    shared, part, query_grad, audio = call(
        queries_kernel,
        "queries",
        [((ALL_ROWS, DH), F32, NEAR), (part_shape, BF, FAR), (six, BF, FAR), (audio_shape, BF, FAR)],
        [audio_len, video_len, queries, keys, unit_vk, video_tables, gathered, freqs, gains],
        smem=2,
        far=5,
        scratch=[
            pltpu.VMEM(queries_shape, BF), pltpu.VMEM(keys_shape, BF), pltpu.VMEM(gathered_shape, BF),
            pltpu.VMEM((3 * DH, DH), F32), pltpu.VMEM(part_shape, BF), pltpu.VMEM(six, BF),
            pltpu.VMEM(audio_shape, BF), dmas(2 + HALF_HEADS), pltpu.SemaphoreType.DMA((3, 3)), pltpu.SemaphoreType.DMA((3, 4)),
        ],
    )

    (merged,) = call(
        back_kernel,
        "back",
        [(tiles, BF, FAR)],
        [part, totals, shared],
        far=1,
        scratch=[pltpu.VMEM(tiles, BF), pltpu.VMEM((24, DH), F32), dmas(3)],
    )
    got = to_group(merged)

    key_own, value_own, other = call(
        keys_kernel,
        "keys",
        [(half, BF), (half, BF), ((3, *half), BF)],
        [video_len, raw_vk, keys, video_tables, query_grad, audio, totals, gains],
        smem=1,
        far=5,
        scratch=[
            pltpu.VMEM(six, BF), pltpu.VMEM(keys_shape, BF), pltpu.VMEM((4 * DH, DH), F32),
            pltpu.VMEM(audio_shape, BF), pltpu.VMEM((2 * DH, DH), F32), pltpu.VMEM((16, DH), F32), dmas(5),
        ],
    )
    other_got = exchange(other)
    grad_vq, grad_vk, grad_vv = call(
        place_kernel, "place", [((DH, F), BF)] * 3, [query_grad, key_own, value_own, other_got]
    )

    audio_half, gain_rows = call(
        audio_kernel,
        "audio",
        [((16, WIDTH), BF), ((2 * clips, 24, DH), F32, FAR)],
        [audio_pos, audio_query, audio_key, freqs, gains, grad_vv, got],
        far=6,
        scratch=[
            places, own_rows, own_rows, pltpu.VMEM((1, DH), F32), pltpu.VMEM((4 * H, DH), F32),
            pltpu.VMEM((2 * clips, 24, DH), F32), dmas(6),
        ],
    )
    gain_got = lax.all_to_all(gain_rows, ("dp", "aseq"), 0, 0, tiled=True)
    audio_got = exchange(audio_half)
    grad_aq, grad_ak, grad_av, sum_vq, sum_vk, sum_aq, sum_ak = call(
        last_kernel,
        "last",
        [((4, F), BF)] * 3 + [((H, DH), F32)] * 4,
        [audio_half, audio_got, gain_got],
    )
    return (
        grad_vq[None],
        grad_vk[None],
        grad_vv[None],
        grad_aq[None],
        grad_ak[None],
        grad_av[None],
        sum_vq.reshape(F),
        sum_vk.reshape(F),
        sum_aq.reshape(F),
        sum_ak.reshape(F),
    )


def solution(mesh):
    video = P("dp", ("vseq", "aseq"), None)
    audio = P("dp", "vseq", None)
    in_specs = (
        (video,) * 4
        + (audio,) * 4
        + (P("dp", ("vseq", "aseq")), P("dp", "vseq"), P("dp"), P("dp"))
        + (P(),) * 4
    )
    out_specs = (video,) * 3 + (audio,) * 3 + (P(),) * 4
    return jax.shard_map(local, mesh=mesh, in_specs=in_specs, out_specs=out_specs, check_vma=False)
```

```python
import functools

import jax
import jax.numpy as jnp
import numpy as np
from jax import lax
from jax.experimental import pallas as pl
from jax.experimental.pallas import tpu as pltpu
from jax.sharding import PartitionSpec as P

H = 12
DH = 128
HALF = DH // 2
EPS = 1e-06
THETA = 10000.0
SCALE = DH ** (-0.5)
BF = jnp.bfloat16
F32 = jnp.float32
VMEM_LIMIT = 24 * 1024 * 1024
HALF_HEADS = H // 2
WIDTH = HALF_HEADS * DH


def frequencies():
    freqs = np.power(np.float64(THETA), -(np.arange(HALF, dtype=np.float64) / HALF))
    return jnp.asarray(np.tile(freqs.astype(np.float32), 2).reshape(1, DH))


def sin_cos(angles):
    turns = jnp.floor(angles * F32(2.0 / np.pi) + 0.5)
    rest = angles - turns * F32(1.5703125)
    rest = rest - turns * F32(4.837512969970703125e-4)
    rest = rest - turns * F32(7.54978995489188216e-8)
    sq = rest * rest
    sine = rest + rest * sq * (
        F32(-1.6666654611e-1) + sq * (F32(8.3321608736e-3) + sq * F32(-1.9515295891e-4))
    )
    cosine = (
        1.0
        - 0.5 * sq
        + sq * sq * (F32(4.166664568298827e-2) + sq * (F32(-1.388731625493765e-3) + sq * F32(2.443315711809948e-5)))
    )
    quarter = turns.astype(jnp.int32)
    odd = (quarter & 1) == 1
    flip = (quarter & 2) == 2
    base_s = jnp.where(odd, cosine, sine)
    base_c = jnp.where(odd, -sine, cosine)
    return jnp.where(flip, -base_s, base_s), jnp.where(flip, -base_c, base_c)


def rotary_tables(pos, freqs):
    sine, cosine = sin_cos(pos * freqs)
    lane = lax.broadcasted_iota(jnp.int32, sine.shape, 1)
    return cosine, jnp.where(lane < HALF, -sine, sine)


def swap(rows):
    return pltpu.roll(rows, HALF, 1)


def unit(rows):
    scale = lax.rsqrt(jnp.sum(rows * rows, axis=-1, keepdims=True) * (1.0 / DH) + EPS)
    return rows * scale, scale


def turn(unit_rows, gain, cosine, sine):
    scaled = unit_rows * gain
    return (scaled * cosine + swap(scaled) * sine).astype(BF)


def raw_unit_and_turn(rows, gain, cosine, sine):
    ones = jnp.ones((DH, DH), BF)
    squares = rows * rows
    high = squares.astype(BF)
    low = (squares - high.astype(F32)).astype(BF)
    total = dot_nn(high, ones) + dot_nn(low, ones)
    swapped = swap(rows)
    yield
    scale = lax.rsqrt(total * (1.0 / DH) + EPS)
    turned = scale * (rows * (gain * cosine) + swapped * (swap(gain) * sine))
    return rows * scale, turned.astype(BF)


def turn_back(grad, cosine, sine):
    return grad * cosine - swap(grad) * sine


def gain_sum(grad, cosine_part, sine_part):
    own = jnp.sum(grad * cosine_part, axis=0, keepdims=True)
    return own + swap(jnp.sum(grad * sine_part, axis=0, keepdims=True))


def norm_back(scaled_grad, unit_rows, scale, gain):
    inner = scaled_grad * gain
    mean = jnp.sum(inner * unit_rows, axis=-1, keepdims=True) * (1.0 / DH)
    return scale * (inner - unit_rows * mean)


def low_rows(shape):
    return (lax.broadcasted_iota(jnp.int32, shape, 0) & 7) < 4


def part_rows(both):
    left, right = both[:DH], both[DH:]
    low = low_rows(left.shape)
    one = jnp.where(low, left, pltpu.roll(right, 4, 0))
    two = jnp.where(low, pltpu.roll(left, DH - 4, 0), right)
    return one, two


def join_rows(one, two):
    low = low_rows(one.shape)
    left = jnp.where(low, one, pltpu.roll(two, 4, 0))
    right = jnp.where(low, pltpu.roll(one, DH - 4, 0), two)
    return left, right


def audio_index():
    row = lax.broadcasted_iota(jnp.int32, (DH, DH), 0)
    inside = row & 7
    return jnp.where(inside < 4, 0, 60) + (row >> 3) * 4 + inside


def dot_nt(a, b):
    return lax.dot_general(a, b, (((1,), (1,)), ((), ())), preferred_element_type=F32)


def dot_tn(a, b):
    return lax.dot_general(a, b, (((0,), (0,)), ((), ())), preferred_element_type=F32)


def dot_nn(a, b):
    return lax.dot_general(a, b, (((1,), (0,)), ((), ())), preferred_element_type=F32)


def lanes(head):
    return pl.ds(pl.multiple_of(head * DH, DH), DH)


def heads_of(core):
    return core * HALF_HEADS


def side_by_side(steps):
    steps, results = list(steps), {}
    running = dict(enumerate(steps))
    while running:
        for at in list(running):
            try:
                next(running[at])
            except StopIteration as end:
                results[at] = end.value
                del running[at]
    return [results[at] for at in range(len(steps))]


def fetch(pairs, done):
    copies = [pltpu.make_async_copy(far, near, done.at[at]) for at, (far, near) in enumerate(pairs)]
    for copy in copies:
        copy.start()
    return copies


def finish(copies):
    for copy in copies:
        copy.wait()


def spread_tile(out, at, rows):
    out[:, at] = jnp.broadcast_to(rows.astype(BF)[None], (32, 8, DH))


def payload_kernel(apos_far, aq_far, ac_far, ak_far, av_far, out_far, out, apos, aq, ac, ak, av, done, sent):
    finish(fetch(((aq_far, aq), (ac_far, ac), (ak_far, ak), (av_far, av), (apos_far, apos)), done))
    base = heads_of(lax.axis_index("aseq"))
    inside = lax.broadcasted_iota(jnp.int32, (8, DH), 0) & 3
    lane = lax.broadcasted_iota(jnp.int32, (8, DH), 1)
    pos = own_places(apos, inside)
    spread_tile(out, 2 * HALF_HEADS, jnp.where(lane < HALF, pos >> 6, pos & 63).astype(F32))
    copies = []
    for j in range(HALF_HEADS):
        columns = lanes(base + j)
        for at, pair in enumerate(((aq, ac), (ak, av))):
            spread_tile(out, 2 * j + at, jnp.concatenate([ref[0, :, columns].astype(F32) for ref in pair], axis=0))
        if j % 2 == 1:
            tiles = slice(2 * j - 2, 2 * j + 2 + (j == HALF_HEADS - 1))
            copies += fetch([(out.at[:, tiles], out_far.at[:, tiles])], sent.at[j // 2 : j // 2 + 1])
    finish(copies)


def own_places(apos, inside):
    early = jnp.where(inside == 0, apos[0, 0], apos[0, 1])
    late = jnp.where(inside == 2, apos[0, 2], apos[0, 3])
    return jnp.where(inside < 2, early, late)


def send_kernel(vq, vk, vv, vc, vpos, out):
    columns = pl.ds(pl.multiple_of(heads_of(1 - lax.axis_index("aseq")) * DH, DH), WIDTH)
    for at, ref in enumerate((vq, vk, vv, vc)):
        out[at * DH : (at + 1) * DH] = ref[:, columns]
    row = lax.broadcasted_iota(jnp.int32, (16, DH), 0)
    pos = jnp.broadcast_to(vpos[...], (16, DH))
    places = jnp.where(row == 0, pos >> 6, pos & 63).astype(F32).astype(BF)
    out[4 * DH : 4 * DH + 16] = jnp.concatenate([places] * HALF_HEADS, axis=1)


def video_mask(vlen, core):
    place = lax.axis_index("vseq") * 2 + core
    row = lax.broadcasted_iota(jnp.int32, (DH, DH), 0)
    return [(row + where * DH < vlen[0]).astype(F32) for where in (place, place + 1 - 2 * core)]


def video_kernel(
    vlen, vq, vk, vv, vc, got, pos_own, freqs, gains,
    keys, queries_far, keys_far, raw_vk_far, unit_vk_far, tables_far,
    queries, raw_vk, unit_vk, tables, done,
):
    core = lax.axis_index("aseq")
    base = heads_of(core)
    masks = video_mask(vlen, core)
    places = got[4 * DH : 4 * DH + 16, 0:DH].astype(F32)
    for at, pos in enumerate((pos_own[...].astype(F32), places[0:1] * 64.0 + places[1:2])):
        rows = slice(at * DH, (at + 1) * DH)
        spread = jnp.transpose(jnp.broadcast_to(pos, (DH, DH)))
        tables[0, rows], tables[1, rows] = rotary_tables(spread, freqs[...])
        tables[2, rows] = masks[at]

    def one_head(j, carry):
        columns = lanes(j)
        own_columns = lanes(base + j)
        for at in range(2):
            rows = slice(at * DH, (at + 1) * DH)
            take = (lambda ref, index: ref[:, own_columns]) if at == 0 else (lambda ref, index: got[index * DH : (index + 1) * DH, columns])
            cosine, sine, mask = tables[0, rows], tables[1, rows], tables[2, rows]
            query, key = take(vq, 0), take(vk, 1)
            queries[j, 0, rows] = query
            raw_vk[j, rows] = key
            keys[j, 1, rows] = take(vv, 2)
            queries[j, 2, rows] = (take(vc, 3).astype(F32) * mask).astype(BF)
            unit_query, _ = unit(query.astype(F32))
            unit_key, _ = unit(key.astype(F32))
            queries[j, 1, rows] = turn(unit_query, gains[pl.ds(base + j, 1), :], cosine, sine)
            keys[j, 0, rows] = turn(unit_key, gains[pl.ds(H + base + j, 1), :], cosine, sine)
            unit_vk[j, rows] = unit_key
        return carry

    lax.fori_loop(0, HALF_HEADS, one_head, 0)
    finish(
        fetch(
            (
                (queries, queries_far), (keys, keys_far), (raw_vk, raw_vk_far), (unit_vk, unit_vk_far),
                (tables, tables_far),
            ),
            done,
        )
    )


def audio_tables(gathered, freqs, alen):
    lane = lax.broadcasted_iota(jnp.int32, (DH, DH), 1)
    apos, _ = part_rows(gathered[:, 2 * HALF_HEADS].astype(F32).reshape(2 * DH, DH))
    apos = jnp.where(lane < HALF, apos * 64.0, apos)
    apos = apos + swap(apos)
    cosine, sine = rotary_tables(apos, freqs[...])
    return cosine, sine, (audio_index() < alen[0]).astype(F32)


def scores_kernel(alen, vlen, gathered, keys, freqs, gains, sums, gathered_far, tables, mask, done):
    copies = fetch([(gathered, gathered_far)], done)
    core = lax.axis_index("aseq")
    base = heads_of(core)
    tables[0], tables[1], tables[2] = audio_tables(gathered, freqs, alen)
    mask[0:DH], mask[DH : 2 * DH] = video_mask(vlen, core)

    def one_head(j):
        aq, ac = part_rows(gathered[:, 2 * j].astype(F32).reshape(2 * DH, DH))
        ac = (ac * tables[2]).astype(BF)
        yield
        _, query = yield from raw_unit_and_turn(aq, gains[pl.ds(2 * H + base + j, 1), :], tables[0], tables[1])
        yield
        cross = dot_nt(keys[j, 0], query)
        dprob = dot_nt(keys[j, 1], ac)
        yield
        cross = jnp.exp(cross * SCALE) * mask[...]
        yield
        return jnp.sum(cross, axis=0, keepdims=True), jnp.sum(cross * dprob, axis=0, keepdims=True)

    found = side_by_side(one_head(j) for j in range(HALF_HEADS))
    rows = [pair[0] for pair in found] + [pair[1] for pair in found]
    for at in range(3):
        block = jnp.concatenate(rows[4 * at : 4 * at + 4], axis=0)
        sums[:, at] = jnp.broadcast_to(block[None], (32, 4, DH))
    finish(copies)


EXPO, DPROB, UNIT_AQ, UNIT_VK, HEAD_ROWS = 0, 2 * DH, 4 * DH, 5 * DH, 7 * DH
TABLES = HALF_HEADS * HEAD_ROWS
COS_V, SIN_V, COS_A, SIN_A, GAINS = TABLES, TABLES + 256, TABLES + 512, TABLES + 640, TABLES + 768
GAIN_VK, GAIN_AQ, GAIN_SUMS, ALL_ROWS = GAINS, GAINS + 8, GAINS + 16, GAINS + 40


def rows_of(j, start, count):
    return pl.ds(pl.multiple_of(j * HEAD_ROWS + start, DH), count)


def queries_kernel(
    alen, vlen, queries_far, keys_far, unit_vk_far, video_far, gathered_far, freqs, gains,
    shared, part_far, grad_far, audio_far,
    queries, keys, gathered, masks, part, grads, audio, done_in, done_step, done_out,
):
    def coming(step):
        heads, rows = pl.ds(2 * step, 2), pl.ds(4 * step, 4)
        pairs = (
            (gathered_far.at[:, rows], gathered.at[:, rows]),
            (keys_far.at[heads], keys.at[heads]),
            (queries_far.at[heads], queries.at[heads]),
        )
        return [pltpu.make_async_copy(far, near, done_step.at[step, at]) for at, (far, near) in enumerate(pairs)]

    places = 2 * HALF_HEADS
    tables = fetch(
        [
            (gathered_far.at[:, places : places + 1], gathered.at[:, places : places + 1]),
            (video_far.at[0 : 2 * 2 * DH], shared.at[COS_V : COS_V + 4 * DH]),
        ],
        done_in,
    )
    for step in range(3):
        for copy in coming(step):
            copy.start()
    units = fetch(
        [(unit_vk_far.at[j], shared.at[j * HEAD_ROWS + UNIT_VK : (j + 1) * HEAD_ROWS]) for j in range(HALF_HEADS)],
        done_in.at[2 : 2 + HALF_HEADS],
    )
    core = lax.axis_index("aseq")
    base = heads_of(core)
    masks[DH : 2 * DH], masks[2 * DH : 3 * DH] = video_mask(vlen, core)
    shared[GAINS:ALL_ROWS] = jnp.zeros((ALL_ROWS - GAINS, DH), F32)
    tables[0].wait()
    shared[COS_A:SIN_A], shared[SIN_A:GAINS], masks[0:DH] = audio_tables(gathered, freqs, alen)
    tables[1].wait()

    def one_head(j):
        cos_v, sin_v, mask_v = shared[COS_V:SIN_V], shared[SIN_V:COS_A], masks[DH : 3 * DH]
        cos_a, sin_a, mask_a = shared[COS_A:SIN_A], shared[SIN_A:GAINS], masks[0:DH]
        gain_aq = gains[pl.ds(2 * H + base + j, 1), :]
        shared[pl.ds(GAIN_VK + j, 1), :] = gains[pl.ds(H + base + j, 1), :]
        shared[pl.ds(GAIN_AQ + j, 1), :] = gain_aq
        aq, ac = part_rows(gathered[:, 2 * j].astype(F32).reshape(2 * DH, DH))
        ak, av = part_rows(gathered[:, 2 * j + 1].astype(F32).reshape(2 * DH, DH))
        av = av.astype(BF)
        ac = (ac * mask_a).astype(BF)
        yield
        unit_ak, _ = unit(ak)
        unit_aq, low_aq = yield from raw_unit_and_turn(aq, gain_aq, cos_a, sin_a)
        unit_vq, scale_vq = unit(queries[j, 0].astype(F32))
        yield
        low_ak = turn(unit_ak, gains[pl.ds(3 * H + base + j, 1), :], cos_a, sin_a)
        audio[j, 0] = low_aq
        audio[j, 1] = ac
        shared[rows_of(j, UNIT_AQ, DH), :] = unit_aq
        yield
        rows, cots = queries[j, 1], queries[j, 2]
        expd = dot_nt(low_ak, rows)
        dp = dot_nt(av, cots)
        yield
        expd = jnp.exp(expd * SCALE) * jnp.concatenate([mask_a, mask_a], axis=1)
        prob = expd * (1.0 / jnp.sum(expd, axis=0, keepdims=True))
        yield
        cross = dot_nt(keys[j, 0], low_aq)
        shared[rows_of(j, DPROB, 2 * DH), :] = dot_nt(keys[j, 1], ac)
        delta = jnp.sum(prob * dp, axis=0, keepdims=True)
        dscore = (prob * (dp - delta)).astype(BF)
        yield
        dq = dot_tn(dscore, low_ak)
        dk = dot_nn(dscore, rows)
        dv = dot_nn(prob.astype(BF), cots)
        yield
        shared[rows_of(j, EXPO, 2 * DH), :] = jnp.exp(cross * SCALE) * mask_v
        yield
        back = turn_back(dq * SCALE, cos_v, sin_v)
        dk = dk * SCALE
        shared[pl.ds(GAIN_SUMS + j, 1), :] = jnp.sum(back * unit_vq, axis=0, keepdims=True)
        yield
        grads[j] = norm_back(back, unit_vq, scale_vq, gains[pl.ds(base + j, 1), :]).astype(BF)
        yield
        sum_ak = jnp.sum(turn_back(dk, cos_a, sin_a) * unit_ak, axis=0, keepdims=True)
        shared[pl.ds(GAIN_SUMS + 18 + j, 1), :] = sum_ak
        return dk, dv

    def going(step):
        heads = pl.ds(2 * step, 2)
        tiles = [(part.at[:, at + step], part_far.at[:, at + step]) for at in (0, 3)]
        pairs = tiles + [(grads.at[heads], grad_far.at[heads]), (audio.at[heads], audio_far.at[heads])]
        return [pltpu.make_async_copy(near, far, done_out.at[step, at]) for at, (near, far) in enumerate(pairs)]

    def pair(step, carry):
        finish(coming(step))
        found = side_by_side(one_head(2 * step + e) for e in range(2))
        for array in range(2):
            left, right = join_rows(found[0][array], found[1][array])
            part[0:16, array * 3 + step] = left.reshape(16, 8, DH).astype(BF)
            part[16:32, array * 3 + step] = right.reshape(16, 8, DH).astype(BF)
        for copy in going(step):
            copy.start()
        return carry

    lax.fori_loop(0, 3, pair, 0)
    finish(units)
    for step in range(3):
        finish(going(step))


def back_kernel(part_far, totals, shared, merged_far, merged, gain_rows, done):
    coming = fetch([(part_far, merged.at[:, 3:9])], done)
    copies = []
    gain_rows[...] = shared[GAIN_SUMS:ALL_ROWS]
    blocks = [jnp.sum(totals[:, at], axis=0) for at in range(3)]
    rows = [blocks[r // 4][r % 4 : r % 4 + 1] for r in range(2 * HALF_HEADS)]

    def one_head(j):
        start = j * HEAD_ROWS
        cos_v, sin_v = shared[COS_V:SIN_V], shared[SIN_V:COS_A]
        cos_a, sin_a = shared[COS_A:SIN_A], shared[SIN_A:GAINS]
        unit_aq, unit_vk = shared[start + UNIT_AQ : start + UNIT_VK], shared[start + UNIT_VK : start + HEAD_ROWS]
        gain_vk, gain_aq = shared[GAIN_VK + j : GAIN_VK + j + 1], shared[GAIN_AQ + j : GAIN_AQ + j + 1]
        vk_cos, vk_sin = unit_vk * cos_v, swap(unit_vk) * sin_v
        aq_cos, aq_sin = unit_aq * cos_a, swap(unit_aq) * sin_a
        low_vk = (vk_cos * gain_vk + vk_sin * swap(gain_vk)).astype(BF)
        low_aq = (aq_cos * gain_aq + aq_sin * swap(gain_aq)).astype(BF)
        yield
        inverse = 1.0 / rows[j]
        delta = rows[HALF_HEADS + j] * inverse
        prob = shared[start + EXPO : start + DPROB] * inverse
        dscore = (prob * (shared[start + DPROB : start + UNIT_AQ] - delta)).astype(BF)
        yield
        dk = dot_nn(dscore, low_aq)
        dq = dot_tn(dscore, low_vk)
        yield
        gain_rows[6 + j : 7 + j, :] = gain_sum(dk, vk_cos, vk_sin) * SCALE
        yield
        dq = dq * SCALE
        gain_rows[12 + j : 13 + j, :] = gain_sum(dq, aq_cos, aq_sin)
        return dq

    found = side_by_side(one_head(j) for j in range(HALF_HEADS))
    for pair in range(3):
        left, right = join_rows(found[2 * pair], found[2 * pair + 1])
        merged[0:16, pair] = left.reshape(16, 8, DH).astype(BF)
        merged[16:32, pair] = right.reshape(16, 8, DH).astype(BF)
    finish(coming)
    copies += fetch([(merged.at[:, 0:9], merged_far.at[:, 0:9])], done.at[1:2])
    for at in range(3):
        spread_tile(merged, 9 + at, gain_rows[8 * at : 8 * at + 8, :])
    copies += fetch([(merged.at[:, 9:12], merged_far.at[:, 9:12])], done.at[2:3])
    finish(copies)


def keys_kernel(
    vlen, raw_vk_far, keys_far, video_far, grad_far, audio_far, totals, gains,
    key_own, value_own, other, raw_vk, keys, tables, audio, mask, sums, done,
):
    copies = fetch(
        (
            (raw_vk_far, raw_vk), (keys_far, keys), (video_far.at[0 : 2 * 2 * DH], tables), (audio_far, audio),
            (grad_far.at[:, DH : 2 * DH], other.at[0]),
        ),
        done,
    )
    core = lax.axis_index("aseq")
    base = heads_of(core)
    mask[0:DH], mask[DH : 2 * DH] = video_mask(vlen, core)
    for at in range(3):
        sums[4 * at : 4 * at + 4, :] = jnp.sum(totals[:, at], axis=0)
    finish(copies)

    def one_head(j, carry):
        cos_v, sin_v = tables[0 : 2 * DH], tables[2 * DH : 4 * DH]
        inverse = 1.0 / sums[pl.ds(j, 1), :]
        delta = sums[pl.ds(HALF_HEADS + j, 1), :] * inverse
        expo = jnp.exp(dot_nt(keys[j, 0], audio[j, 0]) * SCALE) * mask[...]
        prob = expo * inverse
        dscore = (prob * (dot_nt(keys[j, 1], audio[j, 1]) - delta)).astype(BF)
        dk = dot_nn(dscore, audio[j, 0]) * SCALE
        dv = dot_nn(prob.astype(BF), audio[j, 1]).astype(BF)
        unit_vk, scale_vk = unit(raw_vk[j].astype(F32))
        grad = norm_back(turn_back(dk, cos_v, sin_v), unit_vk, scale_vk, gains[pl.ds(H + base + j, 1), :]).astype(BF)
        key_own[j], value_own[j] = grad[:DH], dv[:DH]
        other[1, j], other[2, j] = grad[DH:], dv[DH:]
        return carry

    lax.fori_loop(0, HALF_HEADS, one_head, 0)


def place_kernel(query_own, key_own, value_own, got, grad_vq, grad_vk, grad_vv):
    core = lax.axis_index("aseq")
    for j in range(HALF_HEADS):
        own, other = lanes(heads_of(core) + j), lanes(heads_of(1 - core) + j)
        for at, (mine, grad) in enumerate(((query_own, grad_vq), (key_own, grad_vk), (value_own, grad_vv))):
            grad[:, own] = mine[j, 0:DH]
            grad[:, other] = got[at, j]


def add_peers(got, tiles):
    total = got[0, tiles].astype(F32)
    for v in range(1, 32):
        total = total + got[v, tiles].astype(F32)
    return total


def audio_kernel(
    apos_far, aq_far, ak_far, freqs_far, gains_far, after, got, out, gain_far,
    apos, aq, ak, freqs, gains, gain_out, done,
):
    copies = fetch(((apos_far, apos), (aq_far, aq), (ak_far, ak), (freqs_far, freqs), (gains_far, gains)), done)
    base = heads_of(lax.axis_index("aseq"))
    acc = add_peers(got, slice(9, 12))
    gain_out[...] = jnp.broadcast_to(acc.reshape(1, 24, DH), gain_out.shape)
    sent = fetch([(gain_out, gain_far)], done.at[5:6])
    acc = add_peers(got, slice(0, 9))
    finish(copies)
    pos = own_places(apos, lax.broadcasted_iota(jnp.int32, (8, DH), 0) & 3)
    cosine, sine = rotary_tables(pos.astype(F32), freqs[...])
    low = low_rows((8, DH))

    def rows_back(ref, gain_at, grad, at):
        first = base + 2 * at
        rows = jnp.concatenate([ref[0, :, lanes(first + e)].astype(F32) for e in range(2)], axis=0)
        gain = jnp.where(low, gains[pl.ds(gain_at * H + first, 1), :], gains[pl.ds(gain_at * H + first + 1, 1), :])
        unit_rows, scale = unit(rows)
        return norm_back(turn_back(grad, cosine, sine), unit_rows, scale, gain)

    for at in range(3):
        dq = rows_back(aq, 2, acc[at], at)
        dk = rows_back(ak, 3, acc[3 + at], at)
        dv = acc[6 + at]
        left = jnp.where(low, dq, pltpu.roll(dk, 4, 0))
        right = jnp.where(low, pltpu.roll(dq, 4, 0), dk)
        out[:, 2 * at * DH : (2 * at + 1) * DH] = jnp.concatenate([left, dv], axis=0).astype(BF)
        out[:, (2 * at + 1) * DH : (2 * at + 2) * DH] = jnp.concatenate([right, pltpu.roll(dv, 4, 0)], axis=0).astype(BF)
    finish(sent)


def last_kernel(own, other, gains, grad_aq, grad_ak, grad_av, sum_vq, sum_vk, sum_aq, sum_ak):
    front = lax.axis_index("aseq") == 0
    mine, others = own[...].astype(F32), other[...].astype(F32)
    for at, value in enumerate((jnp.where(front, mine, others), jnp.where(front, others, mine))):
        columns = slice(at * WIDTH, (at + 1) * WIDTH)
        grad_aq[:, columns] = value[0:4].astype(BF)
        grad_ak[:, columns] = value[4:8].astype(BF)
        grad_av[:, columns] = value[8:12].astype(BF)
    for half in range(2):
        total = gains[half]
        for d in range(1, gains.shape[0] // 2):
            total = total + gains[2 * d + half]
        for at, ref in enumerate((sum_vq, sum_vk, sum_aq, sum_ak)):
            ref[6 * half : 6 * half + 6, :] = total[6 * at : 6 * at + 6]


NEAR, FAR = pltpu.VMEM, pltpu.HBM


def call(kernel, name, outs, ins, smem=0, far=0, scratch=()):
    def shape_of(shape, dtype, space=None):
        return jax.ShapeDtypeStruct(shape, dtype) if space is None else space(shape, dtype)

    ins = [pltpu.with_memory_space_constraint(x, FAR) if smem <= at < smem + far else x for at, x in enumerate(ins)]
    return pl.pallas_call(
        kernel,
        name=name,
        out_shape=[shape_of(*out) for out in outs],
        in_specs=[pl.BlockSpec(memory_space=pltpu.SMEM)] * smem
        + [pl.BlockSpec(memory_space=FAR)] * far
        + [pl.BlockSpec(memory_space=NEAR)] * (len(ins) - smem - far),
        out_specs=[pl.BlockSpec(memory_space=FAR if FAR in out else NEAR) for out in outs],
        scratch_shapes=list(scratch),
        compiler_params=pltpu.CompilerParams(vmem_limit_bytes=VMEM_LIMIT),
    )(*ins)


def local(
    video_query, video_key, video_value, video_grad,
    audio_query, audio_key, audio_value, audio_grad,
    video_pos, audio_pos, video_len, audio_len,
    gain_vq, gain_vk, gain_aq, gain_ak,
):
    F = H * DH
    groups = lax.axis_size("vseq")
    clips = lax.axis_size("dp")
    exchange = functools.partial(lax.ppermute, axis_name="aseq", perm=[(0, 1), (1, 0)])
    to_group = functools.partial(lax.all_to_all, axis_name="vseq", split_axis=0, concat_axis=0, tiled=True)
    freqs = frequencies()
    gains = jnp.concatenate([gain_vq, gain_vk, gain_aq, gain_ak]).reshape(4 * H, DH)
    video = [video_query[0], video_key[0], video_value[0], video_grad[0]]
    half = (HALF_HEADS, DH, DH)
    tiles = (groups, 2 * HALF_HEADS, 8, DH)
    six = (HALF_HEADS, 2 * DH, DH)
    queries_shape, keys_shape = (HALF_HEADS, 3, 2 * DH, DH), (HALF_HEADS, 2, 2 * DH, DH)
    gathered_shape = (groups, 2 * HALF_HEADS + 1, 8, DH)
    own_rows = pltpu.VMEM((1, 4, F), BF)
    places = pltpu.SMEM((1, 4), jnp.int32)
    dmas = lambda count: pltpu.SemaphoreType.DMA((count,))

    (payload,) = call(
        payload_kernel,
        "payload",
        [(gathered_shape, BF, FAR)],
        [audio_pos, audio_query, audio_grad, audio_key, audio_value],
        far=5,
        scratch=[pltpu.VMEM(gathered_shape, BF), places] + [own_rows] * 4 + [dmas(5), dmas(3)],
    )
    gathered = to_group(payload)

    (send,) = call(send_kernel, "send", [((4 * DH + 16, WIDTH), BF)], [*video, video_pos])
    video_got = exchange(send)
    keys_near, queries, keys, raw_vk, unit_vk, video_tables = call(
        video_kernel,
        "video",
        [
            (keys_shape, BF, NEAR), (queries_shape, BF, FAR), (keys_shape, BF, FAR), (six, BF, FAR), (six, F32, FAR),
            ((3, 2 * DH, DH), F32, FAR),
        ],
        [video_len, *video, video_got, video_pos, freqs, gains],
        smem=1,
        scratch=[
            pltpu.VMEM(queries_shape, BF), pltpu.VMEM(six, BF), pltpu.VMEM(six, F32),
            pltpu.VMEM((3, 2 * DH, DH), F32), dmas(5),
        ],
    )

    sums, gathered = call(
        scores_kernel,
        "scores",
        [((groups, 3, 4, DH), F32), (gathered_shape, BF, FAR)],
        [audio_len, video_len, gathered, keys_near, freqs, gains],
        smem=2,
        scratch=[pltpu.VMEM((3, DH, DH), F32), pltpu.VMEM((2 * DH, DH), F32), dmas(1)],
    )
    totals = to_group(sums)

    video_tables = video_tables.reshape(6 * DH, DH)
    part_shape, audio_shape = (groups, 6, 8, DH), (HALF_HEADS, 2, DH, DH)
    shared, part, query_grad, audio = call(
        queries_kernel,
        "queries",
        [((ALL_ROWS, DH), F32, NEAR), (part_shape, BF, FAR), (six, BF, FAR), (audio_shape, BF, FAR)],
        [audio_len, video_len, queries, keys, unit_vk, video_tables, gathered, freqs, gains],
        smem=2,
        far=5,
        scratch=[
            pltpu.VMEM(queries_shape, BF), pltpu.VMEM(keys_shape, BF), pltpu.VMEM(gathered_shape, BF),
            pltpu.VMEM((3 * DH, DH), F32), pltpu.VMEM(part_shape, BF), pltpu.VMEM(six, BF),
            pltpu.VMEM(audio_shape, BF), dmas(2 + HALF_HEADS), pltpu.SemaphoreType.DMA((3, 3)), pltpu.SemaphoreType.DMA((3, 4)),
        ],
    )

    (merged,) = call(
        back_kernel,
        "back",
        [(tiles, BF, FAR)],
        [part, totals, shared],
        far=1,
        scratch=[pltpu.VMEM(tiles, BF), pltpu.VMEM((24, DH), F32), dmas(3)],
    )
    got = to_group(merged)

    key_own, value_own, other = call(
        keys_kernel,
        "keys",
        [(half, BF), (half, BF), ((3, *half), BF)],
        [video_len, raw_vk, keys, video_tables, query_grad, audio, totals, gains],
        smem=1,
        far=5,
        scratch=[
            pltpu.VMEM(six, BF), pltpu.VMEM(keys_shape, BF), pltpu.VMEM((4 * DH, DH), F32),
            pltpu.VMEM(audio_shape, BF), pltpu.VMEM((2 * DH, DH), F32), pltpu.VMEM((16, DH), F32), dmas(5),
        ],
    )
    other_got = exchange(other)
    grad_vq, grad_vk, grad_vv = call(
        place_kernel, "place", [((DH, F), BF)] * 3, [query_grad, key_own, value_own, other_got]
    )

    audio_half, gain_rows = call(
        audio_kernel,
        "audio",
        [((16, WIDTH), BF), ((2 * clips, 24, DH), F32, FAR)],
        [audio_pos, audio_query, audio_key, freqs, gains, grad_vv, got],
        far=6,
        scratch=[
            places, own_rows, own_rows, pltpu.VMEM((1, DH), F32), pltpu.VMEM((4 * H, DH), F32),
            pltpu.VMEM((2 * clips, 24, DH), F32), dmas(6),
        ],
    )
    gain_got = lax.all_to_all(gain_rows, ("dp", "aseq"), 0, 0, tiled=True)
    audio_got = exchange(audio_half)
    grad_aq, grad_ak, grad_av, sum_vq, sum_vk, sum_aq, sum_ak = call(
        last_kernel,
        "last",
        [((4, F), BF)] * 3 + [((H, DH), F32)] * 4,
        [audio_half, audio_got, gain_got],
    )
    return (
        grad_vq[None],
        grad_vk[None],
        grad_vv[None],
        grad_aq[None],
        grad_ak[None],
        grad_av[None],
        sum_vq.reshape(F),
        sum_vk.reshape(F),
        sum_aq.reshape(F),
        sum_ak.reshape(F),
    )


def solution(mesh):
    video = P("dp", ("vseq", "aseq"), None)
    audio = P("dp", "vseq", None)
    in_specs = (
        (video,) * 4
        + (audio,) * 4
        + (P("dp", ("vseq", "aseq")), P("dp", "vseq"), P("dp"), P("dp"))
        + (P(),) * 4
    )
    out_specs = (video,) * 3 + (audio,) * 3 + (P(),) * 4
    return jax.shard_map(local, mesh=mesh, in_specs=in_specs, out_specs=out_specs, check_vma=False)
```

```python
import functools

import jax
import jax.numpy as jnp
import numpy as np
from jax import lax
from jax.experimental import pallas as pl
from jax.experimental.pallas import tpu as pltpu
from jax.sharding import PartitionSpec as P

H = 12
DH = 128
HALF = DH // 2
EPS = 1e-06
THETA = 10000.0
SCALE = DH ** (-0.5)
BF = jnp.bfloat16
F32 = jnp.float32
VMEM_LIMIT = 24 * 1024 * 1024
HALF_HEADS = H // 2
WIDTH = HALF_HEADS * DH

PLACES_Z, PLACES_Y = 8, 4
ORDER = [PLACES_Y * (p % PLACES_Z) + p // PLACES_Z for p in range(PLACES_Z * PLACES_Y)]


def frequencies():
    freqs = np.power(np.float64(THETA), -(np.arange(HALF, dtype=np.float64) / HALF))
    return jnp.asarray(np.tile(freqs.astype(np.float32), 2).reshape(1, DH))


def sin_cos(angles):
    turns = jnp.floor(angles * F32(2.0 / np.pi) + 0.5)
    rest = angles - turns * F32(1.5703125)
    rest = rest - turns * F32(4.837512969970703125e-4)
    rest = rest - turns * F32(7.54978995489188216e-8)
    sq = rest * rest
    sine = rest + rest * sq * (
        F32(-1.6666654611e-1) + sq * (F32(8.3321608736e-3) + sq * F32(-1.9515295891e-4))
    )
    cosine = (
        1.0
        - 0.5 * sq
        + sq * sq * (F32(4.166664568298827e-2) + sq * (F32(-1.388731625493765e-3) + sq * F32(2.443315711809948e-5)))
    )
    quarter = turns.astype(jnp.int32)
    odd = (quarter & 1) == 1
    flip = (quarter & 2) == 2
    base_s = jnp.where(odd, cosine, sine)
    base_c = jnp.where(odd, -sine, cosine)
    return jnp.where(flip, -base_s, base_s), jnp.where(flip, -base_c, base_c)


def rotary_tables(pos, freqs):
    sine, cosine = sin_cos(pos * freqs)
    lane = lax.broadcasted_iota(jnp.int32, sine.shape, 1)
    return cosine, jnp.where(lane < HALF, -sine, sine)


def swap(rows):
    return pltpu.roll(rows, HALF, 1)


def unit(rows):
    scale = lax.rsqrt(jnp.sum(rows * rows, axis=-1, keepdims=True) * (1.0 / DH) + EPS)
    return rows * scale, scale


def turn(unit_rows, gain, cosine, sine):
    scaled = unit_rows * gain
    return (scaled * cosine + swap(scaled) * sine).astype(BF)


def raw_unit_and_turn(rows, gain, cosine, sine):
    ones = jnp.ones((DH, DH), BF)
    squares = rows * rows
    high = squares.astype(BF)
    low = (squares - high.astype(F32)).astype(BF)
    total = dot_nn(high, ones) + dot_nn(low, ones)
    swapped = swap(rows)
    yield
    scale = lax.rsqrt(total * (1.0 / DH) + EPS)
    turned = scale * (rows * (gain * cosine) + swapped * (swap(gain) * sine))
    return rows * scale, turned.astype(BF)


def turn_back(grad, cosine, sine):
    return grad * cosine - swap(grad) * sine


def gain_sum(grad, cosine_part, sine_part):
    own = jnp.sum(grad * cosine_part, axis=0, keepdims=True)
    return own + swap(jnp.sum(grad * sine_part, axis=0, keepdims=True))


def norm_back(scaled_grad, unit_rows, scale, gain):
    inner = scaled_grad * gain
    mean = jnp.sum(inner * unit_rows, axis=-1, keepdims=True) * (1.0 / DH)
    return scale * (inner - unit_rows * mean)


def low_rows(shape):
    return (lax.broadcasted_iota(jnp.int32, shape, 0) & 7) < 4


def part_rows(both):
    left, right = both[:DH], both[DH:]
    low = low_rows(left.shape)
    one = jnp.where(low, left, pltpu.roll(right, 4, 0))
    two = jnp.where(low, pltpu.roll(left, DH - 4, 0), right)
    return one, two


def join_rows(one, two):
    low = low_rows(one.shape)
    left = jnp.where(low, one, pltpu.roll(two, 4, 0))
    right = jnp.where(low, pltpu.roll(one, DH - 4, 0), two)
    return left, right


def audio_index():
    row = lax.broadcasted_iota(jnp.int32, (DH, DH), 0)
    at = (row >> 3) + jnp.where((row & 7) < 4, 0, 16)
    return (PLACES_Y * (at & (PLACES_Z - 1)) + (at >> 3)) * 4 + (row & 3)


def dot_nt(a, b):
    return lax.dot_general(a, b, (((1,), (1,)), ((), ())), preferred_element_type=F32)


def dot_tn(a, b):
    return lax.dot_general(a, b, (((0,), (0,)), ((), ())), preferred_element_type=F32)


def dot_nn(a, b):
    return lax.dot_general(a, b, (((1,), (0,)), ((), ())), preferred_element_type=F32)


def lanes(head):
    return pl.ds(pl.multiple_of(head * DH, DH), DH)


def heads_of(core):
    return core * HALF_HEADS


def side_by_side(steps):
    steps, results = list(steps), {}
    running = dict(enumerate(steps))
    while running:
        for at in list(running):
            try:
                next(running[at])
            except StopIteration as end:
                results[at] = end.value
                del running[at]
    return [results[at] for at in range(len(steps))]


def fetch(pairs, done):
    copies = [pltpu.make_async_copy(far, near, done.at[at]) for at, (far, near) in enumerate(pairs)]
    for copy in copies:
        copy.start()
    return copies


def finish(copies):
    for copy in copies:
        copy.wait()


def spread_tile(out, at, rows):
    out[:, at] = jnp.broadcast_to(rows.astype(BF)[None], (32, 8, DH))


def payload_kernel(apos_far, aq_far, ac_far, ak_far, av_far, out_far, out, apos, aq, ac, ak, av, done, sent):
    finish(fetch(((aq_far, aq), (ac_far, ac), (ak_far, ak), (av_far, av), (apos_far, apos)), done))
    base = heads_of(lax.axis_index("aseq"))
    inside = lax.broadcasted_iota(jnp.int32, (8, DH), 0) & 3
    lane = lax.broadcasted_iota(jnp.int32, (8, DH), 1)
    pos = own_places(apos, inside)
    spread_tile(out, 2 * HALF_HEADS, jnp.where(lane < HALF, pos >> 6, pos & 63).astype(F32))
    copies = []
    for j in range(HALF_HEADS):
        columns = lanes(base + j)
        for at, pair in enumerate(((aq, ac), (ak, av))):
            spread_tile(out, 2 * j + at, jnp.concatenate([ref[0, :, columns].astype(F32) for ref in pair], axis=0))
        if j % 2 == 1:
            tiles = slice(2 * j - 2, 2 * j + 2 + (j == HALF_HEADS - 1))
            copies += fetch([(out.at[:, tiles], out_far.at[:, tiles])], sent.at[j // 2 : j // 2 + 1])
    finish(copies)


def own_places(apos, inside):
    early = jnp.where(inside == 0, apos[0, 0], apos[0, 1])
    late = jnp.where(inside == 2, apos[0, 2], apos[0, 3])
    return jnp.where(inside < 2, early, late)


def send_kernel(vq, vk, vv, vc, vpos, out):
    columns = pl.ds(pl.multiple_of(heads_of(1 - lax.axis_index("aseq")) * DH, DH), WIDTH)
    for at, ref in enumerate((vq, vk, vv, vc)):
        out[at * DH : (at + 1) * DH] = ref[:, columns]
    row = lax.broadcasted_iota(jnp.int32, (16, DH), 0)
    pos = jnp.broadcast_to(vpos[...], (16, DH))
    places = jnp.where(row == 0, pos >> 6, pos & 63).astype(F32).astype(BF)
    out[4 * DH : 4 * DH + 16] = jnp.concatenate([places] * HALF_HEADS, axis=1)


def video_mask(vlen, core):
    place = lax.axis_index("vseq") * 2 + core
    row = lax.broadcasted_iota(jnp.int32, (DH, DH), 0)
    return [(row + where * DH < vlen[0]).astype(F32) for where in (place, place + 1 - 2 * core)]


def video_kernel(
    vlen, vq, vk, vv, vc, got, pos_own, freqs, gains,
    keys, queries_far, keys_far, raw_vk_far, unit_vk_far, tables_far,
    queries, raw_vk, unit_vk, tables, done,
):
    core = lax.axis_index("aseq")
    base = heads_of(core)
    masks = video_mask(vlen, core)
    places = got[4 * DH : 4 * DH + 16, 0:DH].astype(F32)
    for at, pos in enumerate((pos_own[...].astype(F32), places[0:1] * 64.0 + places[1:2])):
        rows = slice(at * DH, (at + 1) * DH)
        spread = jnp.transpose(jnp.broadcast_to(pos, (DH, DH)))
        tables[0, rows], tables[1, rows] = rotary_tables(spread, freqs[...])
        tables[2, rows] = masks[at]

    def one_head(j, carry):
        columns = lanes(j)
        own_columns = lanes(base + j)
        for at in range(2):
            rows = slice(at * DH, (at + 1) * DH)
            take = (lambda ref, index: ref[:, own_columns]) if at == 0 else (lambda ref, index: got[index * DH : (index + 1) * DH, columns])
            cosine, sine, mask = tables[0, rows], tables[1, rows], tables[2, rows]
            query, key = take(vq, 0), take(vk, 1)
            queries[j, 0, rows] = query
            raw_vk[j, rows] = key
            keys[j, 1, rows] = take(vv, 2)
            queries[j, 2, rows] = (take(vc, 3).astype(F32) * mask).astype(BF)
            unit_query, _ = unit(query.astype(F32))
            unit_key, _ = unit(key.astype(F32))
            queries[j, 1, rows] = turn(unit_query, gains[pl.ds(base + j, 1), :], cosine, sine)
            keys[j, 0, rows] = turn(unit_key, gains[pl.ds(H + base + j, 1), :], cosine, sine)
            unit_vk[j, rows] = unit_key
        return carry

    lax.fori_loop(0, HALF_HEADS, one_head, 0)
    finish(
        fetch(
            (
                (queries, queries_far), (keys, keys_far), (raw_vk, raw_vk_far), (unit_vk, unit_vk_far),
                (tables, tables_far),
            ),
            done,
        )
    )


def audio_tables(gathered, freqs, alen):
    lane = lax.broadcasted_iota(jnp.int32, (DH, DH), 1)
    apos, _ = part_rows(gathered[:, 2 * HALF_HEADS].astype(F32).reshape(2 * DH, DH))
    apos = jnp.where(lane < HALF, apos * 64.0, apos)
    apos = apos + swap(apos)
    cosine, sine = rotary_tables(apos, freqs[...])
    return cosine, sine, (audio_index() < alen[0]).astype(F32)


def scores_kernel(alen, vlen, gathered, keys, freqs, gains, sums, gathered_far, tables, mask, done):
    copies = fetch([(gathered, gathered_far)], done)
    core = lax.axis_index("aseq")
    base = heads_of(core)
    tables[0], tables[1], tables[2] = audio_tables(gathered, freqs, alen)
    mask[0:DH], mask[DH : 2 * DH] = video_mask(vlen, core)

    def one_head(j):
        aq, ac = part_rows(gathered[:, 2 * j].astype(F32).reshape(2 * DH, DH))
        ac = (ac * tables[2]).astype(BF)
        yield
        _, query = yield from raw_unit_and_turn(aq, gains[pl.ds(2 * H + base + j, 1), :], tables[0], tables[1])
        yield
        cross = dot_nt(keys[j, 0], query)
        dprob = dot_nt(keys[j, 1], ac)
        yield
        cross = jnp.exp(cross * SCALE) * mask[...]
        yield
        return jnp.sum(cross, axis=0, keepdims=True), jnp.sum(cross * dprob, axis=0, keepdims=True)

    found = side_by_side(one_head(j) for j in range(HALF_HEADS))
    rows = [pair[0] for pair in found] + [pair[1] for pair in found]
    for at in range(3):
        block = jnp.concatenate(rows[4 * at : 4 * at + 4], axis=0)
        sums[:, at] = jnp.broadcast_to(block[None], (32, 4, DH))
    finish(copies)


EXPO, DPROB, UNIT_AQ, UNIT_VK, HEAD_ROWS = 0, 2 * DH, 4 * DH, 5 * DH, 7 * DH
TABLES = HALF_HEADS * HEAD_ROWS
COS_V, SIN_V, COS_A, SIN_A, GAINS = TABLES, TABLES + 256, TABLES + 512, TABLES + 640, TABLES + 768
GAIN_VK, GAIN_AQ, GAIN_SUMS, ALL_ROWS = GAINS, GAINS + 8, GAINS + 16, GAINS + 40


def rows_of(j, start, count):
    return pl.ds(pl.multiple_of(j * HEAD_ROWS + start, DH), count)


def queries_kernel(
    alen, vlen, queries_far, keys_far, unit_vk_far, video_far, gathered_far, freqs, gains,
    shared, part_far, grad_far, audio_far,
    queries, keys, gathered, masks, part, grads, audio, done_in, done_step, done_out,
):
    def coming(step):
        heads, rows = pl.ds(2 * step, 2), pl.ds(4 * step, 4)
        pairs = (
            (gathered_far.at[:, rows], gathered.at[:, rows]),
            (keys_far.at[heads], keys.at[heads]),
            (queries_far.at[heads], queries.at[heads]),
        )
        return [pltpu.make_async_copy(far, near, done_step.at[step, at]) for at, (far, near) in enumerate(pairs)]

    places = 2 * HALF_HEADS
    tables = fetch(
        [
            (gathered_far.at[:, places : places + 1], gathered.at[:, places : places + 1]),
            (video_far.at[0 : 2 * 2 * DH], shared.at[COS_V : COS_V + 4 * DH]),
        ],
        done_in,
    )
    for step in range(3):
        for copy in coming(step):
            copy.start()
    units = fetch(
        [(unit_vk_far.at[j], shared.at[j * HEAD_ROWS + UNIT_VK : (j + 1) * HEAD_ROWS]) for j in range(HALF_HEADS)],
        done_in.at[2 : 2 + HALF_HEADS],
    )
    core = lax.axis_index("aseq")
    base = heads_of(core)
    masks[DH : 2 * DH], masks[2 * DH : 3 * DH] = video_mask(vlen, core)
    shared[GAINS:ALL_ROWS] = jnp.zeros((ALL_ROWS - GAINS, DH), F32)
    tables[0].wait()
    shared[COS_A:SIN_A], shared[SIN_A:GAINS], masks[0:DH] = audio_tables(gathered, freqs, alen)
    tables[1].wait()

    def one_head(j):
        cos_v, sin_v, mask_v = shared[COS_V:SIN_V], shared[SIN_V:COS_A], masks[DH : 3 * DH]
        cos_a, sin_a, mask_a = shared[COS_A:SIN_A], shared[SIN_A:GAINS], masks[0:DH]
        gain_aq = gains[pl.ds(2 * H + base + j, 1), :]
        shared[pl.ds(GAIN_VK + j, 1), :] = gains[pl.ds(H + base + j, 1), :]
        shared[pl.ds(GAIN_AQ + j, 1), :] = gain_aq
        aq, ac = part_rows(gathered[:, 2 * j].astype(F32).reshape(2 * DH, DH))
        ak, av = part_rows(gathered[:, 2 * j + 1].astype(F32).reshape(2 * DH, DH))
        av = av.astype(BF)
        ac = (ac * mask_a).astype(BF)
        yield
        unit_ak, _ = unit(ak)
        unit_aq, low_aq = yield from raw_unit_and_turn(aq, gain_aq, cos_a, sin_a)
        unit_vq, scale_vq = unit(queries[j, 0].astype(F32))
        yield
        low_ak = turn(unit_ak, gains[pl.ds(3 * H + base + j, 1), :], cos_a, sin_a)
        audio[j, 0] = low_aq
        audio[j, 1] = ac
        shared[rows_of(j, UNIT_AQ, DH), :] = unit_aq
        yield
        rows, cots = queries[j, 1], queries[j, 2]
        expd = dot_nt(low_ak, rows)
        dp = dot_nt(av, cots)
        yield
        expd = jnp.exp(expd * SCALE) * jnp.concatenate([mask_a, mask_a], axis=1)
        prob = expd * (1.0 / jnp.sum(expd, axis=0, keepdims=True))
        yield
        cross = dot_nt(keys[j, 0], low_aq)
        shared[rows_of(j, DPROB, 2 * DH), :] = dot_nt(keys[j, 1], ac)
        delta = jnp.sum(prob * dp, axis=0, keepdims=True)
        dscore = (prob * (dp - delta)).astype(BF)
        yield
        dq = dot_tn(dscore, low_ak)
        dk = dot_nn(dscore, rows)
        dv = dot_nn(prob.astype(BF), cots)
        yield
        shared[rows_of(j, EXPO, 2 * DH), :] = jnp.exp(cross * SCALE) * mask_v
        yield
        back = turn_back(dq * SCALE, cos_v, sin_v)
        dk = dk * SCALE
        shared[pl.ds(GAIN_SUMS + j, 1), :] = jnp.sum(back * unit_vq, axis=0, keepdims=True)
        yield
        grads[j] = norm_back(back, unit_vq, scale_vq, gains[pl.ds(base + j, 1), :]).astype(BF)
        yield
        sum_ak = jnp.sum(turn_back(dk, cos_a, sin_a) * unit_ak, axis=0, keepdims=True)
        shared[pl.ds(GAIN_SUMS + 18 + j, 1), :] = sum_ak
        return dk, dv

    def going(step):
        heads = pl.ds(2 * step, 2)
        tiles = [(part.at[:, at + step], part_far.at[:, at + step]) for at in (0, 3)]
        pairs = tiles + [(grads.at[heads], grad_far.at[heads]), (audio.at[heads], audio_far.at[heads])]
        return [pltpu.make_async_copy(near, far, done_out.at[step, at]) for at, (near, far) in enumerate(pairs)]

    def pair(step, carry):
        finish(coming(step))
        found = side_by_side(one_head(2 * step + e) for e in range(2))
        for array in range(2):
            left, right = join_rows(found[0][array], found[1][array])
            part[0:16, array * 3 + step] = left.reshape(16, 8, DH).astype(BF)
            part[16:32, array * 3 + step] = right.reshape(16, 8, DH).astype(BF)
        for copy in going(step):
            copy.start()
        return carry

    lax.fori_loop(0, 3, pair, 0)
    finish(units)
    for step in range(3):
        finish(going(step))


def back_kernel(part_far, totals, shared, merged_far, merged, gain_rows, done):
    coming = fetch([(part_far, merged.at[:, 3:9])], done)
    copies = []
    gain_rows[...] = shared[GAIN_SUMS:ALL_ROWS]
    blocks = [jnp.sum(totals[:, at], axis=0) for at in range(3)]
    rows = [blocks[r // 4][r % 4 : r % 4 + 1] for r in range(2 * HALF_HEADS)]

    def one_head(j):
        start = j * HEAD_ROWS
        cos_v, sin_v = shared[COS_V:SIN_V], shared[SIN_V:COS_A]
        cos_a, sin_a = shared[COS_A:SIN_A], shared[SIN_A:GAINS]
        unit_aq, unit_vk = shared[start + UNIT_AQ : start + UNIT_VK], shared[start + UNIT_VK : start + HEAD_ROWS]
        gain_vk, gain_aq = shared[GAIN_VK + j : GAIN_VK + j + 1], shared[GAIN_AQ + j : GAIN_AQ + j + 1]
        vk_cos, vk_sin = unit_vk * cos_v, swap(unit_vk) * sin_v
        aq_cos, aq_sin = unit_aq * cos_a, swap(unit_aq) * sin_a
        low_vk = (vk_cos * gain_vk + vk_sin * swap(gain_vk)).astype(BF)
        low_aq = (aq_cos * gain_aq + aq_sin * swap(gain_aq)).astype(BF)
        yield
        inverse = 1.0 / rows[j]
        delta = rows[HALF_HEADS + j] * inverse
        prob = shared[start + EXPO : start + DPROB] * inverse
        dscore = (prob * (shared[start + DPROB : start + UNIT_AQ] - delta)).astype(BF)
        yield
        dk = dot_nn(dscore, low_aq)
        dq = dot_tn(dscore, low_vk)
        yield
        gain_rows[6 + j : 7 + j, :] = gain_sum(dk, vk_cos, vk_sin) * SCALE
        yield
        dq = dq * SCALE
        gain_rows[12 + j : 13 + j, :] = gain_sum(dq, aq_cos, aq_sin)
        return dq

    found = side_by_side(one_head(j) for j in range(HALF_HEADS))
    for pair in range(3):
        left, right = join_rows(found[2 * pair], found[2 * pair + 1])
        merged[0:16, pair] = left.reshape(16, 8, DH).astype(BF)
        merged[16:32, pair] = right.reshape(16, 8, DH).astype(BF)
    finish(coming)
    copies += fetch([(merged.at[:, 0:9], merged_far.at[:, 0:9])], done.at[1:2])
    for at in range(3):
        spread_tile(merged, 9 + at, gain_rows[8 * at : 8 * at + 8, :])
    copies += fetch([(merged.at[:, 9:12], merged_far.at[:, 9:12])], done.at[2:3])
    finish(copies)


def keys_kernel(
    vlen, raw_vk_far, keys_far, video_far, grad_far, audio_far, totals, gains,
    key_own, value_own, other, raw_vk, keys, tables, audio, mask, sums, done,
):
    copies = fetch(
        (
            (raw_vk_far, raw_vk), (keys_far, keys), (video_far.at[0 : 2 * 2 * DH], tables), (audio_far, audio),
            (grad_far.at[:, DH : 2 * DH], other.at[0]),
        ),
        done,
    )
    core = lax.axis_index("aseq")
    base = heads_of(core)
    mask[0:DH], mask[DH : 2 * DH] = video_mask(vlen, core)
    for at in range(3):
        sums[4 * at : 4 * at + 4, :] = jnp.sum(totals[:, at], axis=0)
    finish(copies)

    def one_head(j, carry):
        cos_v, sin_v = tables[0 : 2 * DH], tables[2 * DH : 4 * DH]
        inverse = 1.0 / sums[pl.ds(j, 1), :]
        delta = sums[pl.ds(HALF_HEADS + j, 1), :] * inverse
        expo = jnp.exp(dot_nt(keys[j, 0], audio[j, 0]) * SCALE) * mask[...]
        prob = expo * inverse
        dscore = (prob * (dot_nt(keys[j, 1], audio[j, 1]) - delta)).astype(BF)
        dk = dot_nn(dscore, audio[j, 0]) * SCALE
        dv = dot_nn(prob.astype(BF), audio[j, 1]).astype(BF)
        unit_vk, scale_vk = unit(raw_vk[j].astype(F32))
        grad = norm_back(turn_back(dk, cos_v, sin_v), unit_vk, scale_vk, gains[pl.ds(H + base + j, 1), :]).astype(BF)
        key_own[j], value_own[j] = grad[:DH], dv[:DH]
        other[1, j], other[2, j] = grad[DH:], dv[DH:]
        return carry

    lax.fori_loop(0, HALF_HEADS, one_head, 0)


def place_kernel(query_own, key_own, value_own, got, grad_vq, grad_vk, grad_vv):
    core = lax.axis_index("aseq")
    for j in range(HALF_HEADS):
        own, other = lanes(heads_of(core) + j), lanes(heads_of(1 - core) + j)
        for at, (mine, grad) in enumerate(((query_own, grad_vq), (key_own, grad_vk), (value_own, grad_vv))):
            grad[:, own] = mine[j, 0:DH]
            grad[:, other] = got[at, j]


def add_peers(got, tiles):
    total = got[0, tiles].astype(F32)
    for v in range(1, 32):
        total = total + got[v, tiles].astype(F32)
    return total


def audio_kernel(
    apos_far, aq_far, ak_far, freqs_far, gains_far, after, got, out, gain_far,
    apos, aq, ak, freqs, gains, gain_out, done,
):
    copies = fetch(((apos_far, apos), (aq_far, aq), (ak_far, ak), (freqs_far, freqs), (gains_far, gains)), done)
    base = heads_of(lax.axis_index("aseq"))
    acc = add_peers(got, slice(9, 12))
    gain_out[...] = jnp.broadcast_to(acc.reshape(1, 24, DH), gain_out.shape)
    sent = fetch([(gain_out, gain_far)], done.at[5:6])
    acc = add_peers(got, slice(0, 9))
    finish(copies)
    pos = own_places(apos, lax.broadcasted_iota(jnp.int32, (8, DH), 0) & 3)
    cosine, sine = rotary_tables(pos.astype(F32), freqs[...])
    low = low_rows((8, DH))

    def rows_back(ref, gain_at, grad, at):
        first = base + 2 * at
        rows = jnp.concatenate([ref[0, :, lanes(first + e)].astype(F32) for e in range(2)], axis=0)
        gain = jnp.where(low, gains[pl.ds(gain_at * H + first, 1), :], gains[pl.ds(gain_at * H + first + 1, 1), :])
        unit_rows, scale = unit(rows)
        return norm_back(turn_back(grad, cosine, sine), unit_rows, scale, gain)

    for at in range(3):
        dq = rows_back(aq, 2, acc[at], at)
        dk = rows_back(ak, 3, acc[3 + at], at)
        dv = acc[6 + at]
        left = jnp.where(low, dq, pltpu.roll(dk, 4, 0))
        right = jnp.where(low, pltpu.roll(dq, 4, 0), dk)
        out[:, 2 * at * DH : (2 * at + 1) * DH] = jnp.concatenate([left, dv], axis=0).astype(BF)
        out[:, (2 * at + 1) * DH : (2 * at + 2) * DH] = jnp.concatenate([right, pltpu.roll(dv, 4, 0)], axis=0).astype(BF)
    finish(sent)


def last_kernel(own, other, gains, grad_aq, grad_ak, grad_av, sum_vq, sum_vk, sum_aq, sum_ak):
    front = lax.axis_index("aseq") == 0
    mine, others = own[...].astype(F32), other[...].astype(F32)
    for at, value in enumerate((jnp.where(front, mine, others), jnp.where(front, others, mine))):
        columns = slice(at * WIDTH, (at + 1) * WIDTH)
        grad_aq[:, columns] = value[0:4].astype(BF)
        grad_ak[:, columns] = value[4:8].astype(BF)
        grad_av[:, columns] = value[8:12].astype(BF)
    for half in range(2):
        total = gains[half]
        for d in range(1, gains.shape[0] // 2):
            total = total + gains[2 * d + half]
        for at, ref in enumerate((sum_vq, sum_vk, sum_aq, sum_ak)):
            ref[6 * half : 6 * half + 6, :] = total[6 * at : 6 * at + 6]


NEAR, FAR = pltpu.VMEM, pltpu.HBM


def call(kernel, name, outs, ins, smem=0, far=0, scratch=()):
    def shape_of(shape, dtype, space=None):
        return jax.ShapeDtypeStruct(shape, dtype) if space is None else space(shape, dtype)

    ins = [pltpu.with_memory_space_constraint(x, FAR) if smem <= at < smem + far else x for at, x in enumerate(ins)]
    return pl.pallas_call(
        kernel,
        name=name,
        out_shape=[shape_of(*out) for out in outs],
        in_specs=[pl.BlockSpec(memory_space=pltpu.SMEM)] * smem
        + [pl.BlockSpec(memory_space=FAR)] * far
        + [pl.BlockSpec(memory_space=NEAR)] * (len(ins) - smem - far),
        out_specs=[pl.BlockSpec(memory_space=FAR if FAR in out else NEAR) for out in outs],
        scratch_shapes=list(scratch),
        compiler_params=pltpu.CompilerParams(vmem_limit_bytes=VMEM_LIMIT),
    )(*ins)


def local(
    video_query, video_key, video_value, video_grad,
    audio_query, audio_key, audio_value, audio_grad,
    video_pos, audio_pos, video_len, audio_len,
    gain_vq, gain_vk, gain_aq, gain_ak,
):
    F = H * DH
    groups = lax.axis_size("vseq")
    clips = lax.axis_size("dp")
    exchange = functools.partial(lax.ppermute, axis_name="aseq", perm=[(0, 1), (1, 0)])
    to_group = functools.partial(
        lax.all_to_all, axis_name="vseq", split_axis=0, concat_axis=0, axis_index_groups=[ORDER], tiled=True
    )
    freqs = frequencies()
    gains = jnp.concatenate([gain_vq, gain_vk, gain_aq, gain_ak]).reshape(4 * H, DH)
    video = [video_query[0], video_key[0], video_value[0], video_grad[0]]
    half = (HALF_HEADS, DH, DH)
    tiles = (groups, 2 * HALF_HEADS, 8, DH)
    six = (HALF_HEADS, 2 * DH, DH)
    queries_shape, keys_shape = (HALF_HEADS, 3, 2 * DH, DH), (HALF_HEADS, 2, 2 * DH, DH)
    gathered_shape = (groups, 2 * HALF_HEADS + 1, 8, DH)
    own_rows = pltpu.VMEM((1, 4, F), BF)
    places = pltpu.SMEM((1, 4), jnp.int32)
    dmas = lambda count: pltpu.SemaphoreType.DMA((count,))

    (payload,) = call(
        payload_kernel,
        "payload",
        [(gathered_shape, BF, FAR)],
        [audio_pos, audio_query, audio_grad, audio_key, audio_value],
        far=5,
        scratch=[pltpu.VMEM(gathered_shape, BF), places] + [own_rows] * 4 + [dmas(5), dmas(3)],
    )
    gathered = to_group(payload)

    (send,) = call(send_kernel, "send", [((4 * DH + 16, WIDTH), BF)], [*video, video_pos])
    video_got = exchange(send)
    keys_near, queries, keys, raw_vk, unit_vk, video_tables = call(
        video_kernel,
        "video",
        [
            (keys_shape, BF, NEAR), (queries_shape, BF, FAR), (keys_shape, BF, FAR), (six, BF, FAR), (six, F32, FAR),
            ((3, 2 * DH, DH), F32, FAR),
        ],
        [video_len, *video, video_got, video_pos, freqs, gains],
        smem=1,
        scratch=[
            pltpu.VMEM(queries_shape, BF), pltpu.VMEM(six, BF), pltpu.VMEM(six, F32),
            pltpu.VMEM((3, 2 * DH, DH), F32), dmas(5),
        ],
    )

    sums, gathered = call(
        scores_kernel,
        "scores",
        [((groups, 3, 4, DH), F32), (gathered_shape, BF, FAR)],
        [audio_len, video_len, gathered, keys_near, freqs, gains],
        smem=2,
        scratch=[pltpu.VMEM((3, DH, DH), F32), pltpu.VMEM((2 * DH, DH), F32), dmas(1)],
    )
    totals = to_group(sums)

    video_tables = video_tables.reshape(6 * DH, DH)
    part_shape, audio_shape = (groups, 6, 8, DH), (HALF_HEADS, 2, DH, DH)
    shared, part, query_grad, audio = call(
        queries_kernel,
        "queries",
        [((ALL_ROWS, DH), F32, NEAR), (part_shape, BF, FAR), (six, BF, FAR), (audio_shape, BF, FAR)],
        [audio_len, video_len, queries, keys, unit_vk, video_tables, gathered, freqs, gains],
        smem=2,
        far=5,
        scratch=[
            pltpu.VMEM(queries_shape, BF), pltpu.VMEM(keys_shape, BF), pltpu.VMEM(gathered_shape, BF),
            pltpu.VMEM((3 * DH, DH), F32), pltpu.VMEM(part_shape, BF), pltpu.VMEM(six, BF),
            pltpu.VMEM(audio_shape, BF), dmas(2 + HALF_HEADS), pltpu.SemaphoreType.DMA((3, 3)), pltpu.SemaphoreType.DMA((3, 4)),
        ],
    )

    (merged,) = call(
        back_kernel,
        "back",
        [(tiles, BF, FAR)],
        [part, totals, shared],
        far=1,
        scratch=[pltpu.VMEM(tiles, BF), pltpu.VMEM((24, DH), F32), dmas(3)],
    )
    got = to_group(merged)

    key_own, value_own, other = call(
        keys_kernel,
        "keys",
        [(half, BF), (half, BF), ((3, *half), BF)],
        [video_len, raw_vk, keys, video_tables, query_grad, audio, totals, gains],
        smem=1,
        far=5,
        scratch=[
            pltpu.VMEM(six, BF), pltpu.VMEM(keys_shape, BF), pltpu.VMEM((4 * DH, DH), F32),
            pltpu.VMEM(audio_shape, BF), pltpu.VMEM((2 * DH, DH), F32), pltpu.VMEM((16, DH), F32), dmas(5),
        ],
    )
    other_got = exchange(other)
    grad_vq, grad_vk, grad_vv = call(
        place_kernel, "place", [((DH, F), BF)] * 3, [query_grad, key_own, value_own, other_got]
    )

    audio_half, gain_rows = call(
        audio_kernel,
        "audio",
        [((16, WIDTH), BF), ((2 * clips, 24, DH), F32, FAR)],
        [audio_pos, audio_query, audio_key, freqs, gains, grad_vv, got],
        far=6,
        scratch=[
            places, own_rows, own_rows, pltpu.VMEM((1, DH), F32), pltpu.VMEM((4 * H, DH), F32),
            pltpu.VMEM((2 * clips, 24, DH), F32), dmas(6),
        ],
    )
    gain_got = lax.all_to_all(gain_rows, ("dp", "aseq"), 0, 0, tiled=True)
    audio_got = exchange(audio_half)
    grad_aq, grad_ak, grad_av, sum_vq, sum_vk, sum_aq, sum_ak = call(
        last_kernel,
        "last",
        [((4, F), BF)] * 3 + [((H, DH), F32)] * 4,
        [audio_half, audio_got, gain_got],
    )
    return (
        grad_vq[None],
        grad_vk[None],
        grad_vv[None],
        grad_aq[None],
        grad_ak[None],
        grad_av[None],
        sum_vq.reshape(F),
        sum_vk.reshape(F),
        sum_aq.reshape(F),
        sum_ak.reshape(F),
    )


def solution(mesh):
    video = P("dp", ("vseq", "aseq"), None)
    audio = P("dp", "vseq", None)
    in_specs = (
        (video,) * 4
        + (audio,) * 4
        + (P("dp", ("vseq", "aseq")), P("dp", "vseq"), P("dp"), P("dp"))
        + (P(),) * 4
    )
    out_specs = (video,) * 3 + (audio,) * 3 + (P(),) * 4
    return jax.shard_map(local, mesh=mesh, in_specs=in_specs, out_specs=out_specs, check_vma=False)
```
